32 devices in a mesh: rep: 2 (over y), grp: 8 (over z, x), tp: 2 (over core).
Axes of the slice: x: 2, y: 2, z: 4, core: 2. Of those that a mesh axis runs over, the one named last changes fastest.
Arguments:
- counts: int32 [16], P(('rep', 'grp')), parts along dimension 0, may hold values from 1 to 8, as said below
- hop_offsets: int32 [128], P(('rep', 'grp')), parts along dimension 0, may hold values from -2 to 2, as said below
- write_pos: int32 [128], P(('rep', 'grp')), parts along dimension 0, may hold values from 0 to 123
- kv_cache: bfloat16 [128, 2, 128, 1024], P(('rep', 'grp'), None, None, 'tp'), parts along dimension 0, may hold values from -27 to 27
- queries: bfloat16 [128, 2, 8192], P(('rep', 'grp'), None, 'tp'), parts along dimension 0, may hold values from -6 to 6
- fresh_kv: bfloat16 [128, 2, 2, 1024], P(('rep', 'grp'), None, None, 'tp'), parts along dimension 0, may hold values from -6 to 6
Outputs:
- new_cache: bfloat16 [128, 2, 128, 1024], P(('rep', 'grp'), None, None, 'tp'), parts along dimension 0
- attended: bfloat16 [128, 2, 8192], P(('rep', 'grp'), None, 'tp'), parts along dimension 0
- served: int32 [16], P('rep'), parts along dimension 0
The draws below stay inside these ranges and needn't reach their ends.
There are 2 independent parts, one for each index of `rep`. The reference program is written for one: setup_inputs(seed, part) draws one part's arguments, and reference() takes and returns one part's arrays. A program takes and returns all parts, laid end to end along the dimension named above; each array names one. Nothing has to cross between parts.
Inputs may be any that keep to these rules, and one draw needn't show every extreme that they name: `counts`: live streams fill a group's first slots; some group holds 8 streams; groups that send hold 8 streams, the others 1 or 2. `hop_offsets`: zero for empty slots and staying streams. A group sends at most one stream with each offset, and no group holds more than 8 streams after the move; offsets -2 and 2 occur.
All inputs are finite; a program needn't handle non-finite values.
Results may differ from the reference program's by a relative error of at most 0.0049.
Values may be sent and summed in bfloat16 or wider, within the bound.
No kernel may reach another device: no remote copies, remote signals or barrier semaphores. Data moves between devices by JAX's collectives and lax.ppermute only.
A program may use at most 64 MiB of HBM per device.

```python
import jax
import jax.numpy as jnp
from jax import lax

HEADS = 64
KV_HEADS = 8
HEAD_DIM = 128
SINK = 4
REACH = 2
CACHE = 128
SLOTS = 8
WINDOW = 124
GROUPS = 8
STREAMS = 64


def migration_plan(key):
    base_key = jax.random.fold_in(key, 5)
    key_first = jax.random.fold_in(base_key, 0)
    key_light = jax.random.fold_in(base_key, 2)
    key_order = jax.random.fold_in(base_key, 3)
    group_index = jnp.arange(GROUPS)
    first_heavy = jax.random.randint(key_first, (), 0, 5)
    residue = (group_index - first_heavy) % 5
    is_heavy = ((residue == 0) | (residue == 2)) & (group_index < GROUPS - 2)
    light_count = jax.random.randint(key_light, (GROUPS,), 1, 3)
    count_table = jnp.where(is_heavy, SLOTS, light_count).astype(jnp.int32)
    slot_index = jnp.arange(SLOTS)
    order_scores = jax.random.randint(key_order, (GROUPS, SLOTS), 0, 1 << 20) * SLOTS + slot_index[None, :]
    slot_order = jnp.argsort(order_scores, axis=1)
    hop_table = jnp.zeros((GROUPS, SLOTS), jnp.int32)
    offsets = [offset for offset in range(-REACH, REACH + 1) if offset != 0]
    for position, offset in enumerate(offsets):
        chosen = (slot_order[:, position:position + 1] == slot_index[None, :]) & is_heavy[:, None]
        hop_table = hop_table + jnp.where(chosen, offset, 0).astype(jnp.int32)
    return (count_table, hop_table.reshape(-1))


def draw_counts(key, part):
    return migration_plan(key)[0]


def draw_hop_offsets(key, part):
    return migration_plan(key)[1]


def draw_kv_cache(key, part):
    key_values = jax.random.fold_in(jax.random.fold_in(key, 21), 0)
    shape = (STREAMS, 2, CACHE, KV_HEADS * HEAD_DIM)
    values_drawn = jnp.clip(jax.random.normal(key_values, shape, jnp.float32), -6.0, 6.0)
    return values_drawn.astype(jnp.bfloat16)


def draw_queries(key, part):
    key_values = jax.random.fold_in(jax.random.fold_in(key, 31), 0)
    shape = (STREAMS, 2, HEADS * HEAD_DIM)
    values_drawn = jnp.clip(jax.random.normal(key_values, shape, jnp.float32), -6.0, 6.0)
    return values_drawn.astype(jnp.bfloat16)


def with_ends(drawn, key, low, top_value):
    shape = drawn.shape
    place = [jax.random.randint(jax.random.fold_in(key, axis), (), 0, shape[axis]) for axis in range(len(shape))]
    drawn = drawn.at[tuple(place)].set(low)
    longest = shape.index(max(shape))
    place[longest] = (place[longest] + 1) % shape[longest]
    return drawn.at[tuple(place)].set(top_value)


def steps_of(rng, dims, pieces, least, largest):
    gain = 1.0
    for axis_at, parts in pieces:
        steps = jax.random.uniform(jax.random.fold_in(jax.random.fold_in(rng, 6), axis_at), (parts,), jnp.float32, least / len(pieces), largest / len(pieces))
        gain = gain * jnp.repeat(jnp.exp(steps), dims[axis_at] // parts).reshape((-1,) + (1,) * (len(dims) - 1 - axis_at))
    return gain


def scatter_about(own_key, shape, width, most, cuts=(), kind=jnp.bfloat16):
    gain = steps_of(own_key, shape, cuts, -0.22, 0.18) if cuts else 1.0
    entries = jax.random.normal(own_key, shape, jnp.float32) * width * gain
    return jnp.minimum(jnp.maximum(entries, -most), most).astype(kind)


def setup_inputs(seed: int = 0, part: int = 0) -> dict:
    key_of = jax.random.split(jax.random.key(seed), 7)
    part_splits = jax.random.split(jax.random.fold_in(key_of[6], part), 7)
    counts = draw_counts(jax.random.fold_in(jax.random.fold_in(key_of[6], part), 71), part)
    hop_offsets = draw_hop_offsets(jax.random.fold_in(jax.random.fold_in(key_of[6], part), 71), part)
    write_pos = with_ends(jax.random.randint(part_splits[2], (STREAMS,), 0, WINDOW), jax.random.fold_in(part_splits[2], 1), 0, WINDOW - 1).astype(jnp.int32)
    kv_cache = draw_kv_cache(jax.random.fold_in(jax.random.fold_in(key_of[6], part), 71), part)
    queries = draw_queries(jax.random.fold_in(jax.random.fold_in(key_of[6], part), 71), part)
    fresh_kv = scatter_about(part_splits[5], (STREAMS, 2, 2, KV_HEADS * HEAD_DIM), 1.0, 6.0, ((0, 8), (3, 2)))
    return dict(counts=counts, hop_offsets=hop_offsets, write_pos=write_pos, kv_cache=kv_cache, queries=queries, fresh_kv=fresh_kv)


def decode_rows(cache_rows, positions, query_rows, fresh_rows):
    row_count, _, cache_len, kv_width = cache_rows.shape
    group_count = kv_width // HEAD_DIM
    head_count = query_rows.shape[-1] // HEAD_DIM
    group_size = head_count // group_count
    window = cache_len - SINK
    columns = jnp.arange(cache_len, dtype=jnp.int32)
    outputs = []
    current = cache_rows
    for step_index in range(2):
        target = (SINK + (positions + step_index) % window).astype(jnp.int32)
        row_hit = (columns[None, :] == target[:, None])[:, None, :, None]
        current = jnp.where(row_hit, fresh_rows[:, :, step_index][:, :, None, :], current)
        key_rows = current[:, 0].reshape(row_count, cache_len, group_count, HEAD_DIM).astype(jnp.float32)
        values = current[:, 1].reshape(row_count, cache_len, group_count, HEAD_DIM).astype(jnp.float32)
        query_now = query_rows[:, step_index].reshape(row_count, group_count, group_size, HEAD_DIM).astype(jnp.float32)
        scores = jnp.einsum("rgkd,rlgd->rgkl", query_now, key_rows, precision=lax.Precision.HIGHEST) * (HEAD_DIM ** -0.5)
        weights = jax.nn.softmax(scores, axis=-1).astype(jnp.bfloat16)
        mixed_heads = jnp.einsum("rgkl,rlgd->rgkd", weights.astype(jnp.float32), values, precision=lax.Precision.HIGHEST)
        outputs.append(mixed_heads.astype(jnp.bfloat16).reshape(row_count, head_count * HEAD_DIM))
    return current, jnp.stack(outputs, axis=1)


def reference(counts, hop_offsets, write_pos, kv_cache, queries, fresh_kv):
    slot_index = jnp.arange(SLOTS, dtype=jnp.int32)
    group_index = jnp.arange(GROUPS, dtype=jnp.int32)
    is_live = slot_index[None, :] < counts[:, None]
    moving = jnp.where(is_live, hop_offsets.reshape(GROUPS, SLOTS), 0).astype(jnp.int32)
    staying = is_live & (moving == 0)
    stay_rank = jnp.cumsum(staying.astype(jnp.int32), axis=1).astype(jnp.int32) - 1
    running = jnp.sum(staying.astype(jnp.int32), axis=1).astype(jnp.int32)
    stream_ids = group_index[:, None] * SLOTS + slot_index[None, :]
    dest_parts = [jnp.where(staying, stay_rank, -1).astype(jnp.int32)]
    source_parts = [stream_ids]
    offsets = [offset for offset in range(-REACH, REACH + 1) if offset != 0]
    for offset in offsets:
        chosen = moving == offset
        present = jnp.any(chosen, axis=1)
        picked = jnp.sum(jnp.where(chosen, slot_index[None, :], 0), axis=1).astype(jnp.int32)
        incoming = jnp.roll(present, offset)
        anchor = jnp.roll(group_index * SLOTS + picked, offset).astype(jnp.int32)
        dest_parts.append(jnp.where(incoming, running, -1).astype(jnp.int32)[:, None])
        source_parts.append(anchor[:, None])
        running = running + incoming.astype(jnp.int32)
    pool_dest = jnp.concatenate(dest_parts, axis=1)
    pool_source = jnp.concatenate(source_parts, axis=1)
    matches = pool_dest[:, None, :] == slot_index[None, :, None]
    filled = jnp.any(matches, axis=2).reshape(-1)
    source = jnp.sum(jnp.where(matches, pool_source[:, None, :], 0), axis=2).astype(jnp.int32).reshape(-1)
    placed = jnp.take(kv_cache, source, axis=0)
    placed_pos = jnp.take(write_pos, source).astype(jnp.int32)

    def per_group(operands):
        return decode_rows(operands[0], operands[1], operands[2], operands[3])

    shaped = (placed.reshape((GROUPS, SLOTS) + placed.shape[1:]),
              placed_pos.reshape(GROUPS, SLOTS),
              queries.reshape((GROUPS, SLOTS) + queries.shape[1:]),
              fresh_kv.reshape((GROUPS, SLOTS) + fresh_kv.shape[1:]))
    cache_out, attention_out = lax.map(per_group, shaped)
    cache_out = cache_out.reshape(kv_cache.shape)
    attention_out = attention_out.reshape(queries.shape)
    new_cache = jnp.where(filled[:, None, None, None], cache_out, jnp.zeros((), jnp.bfloat16))
    attended = jnp.where(filled[:, None, None], attention_out, jnp.zeros((), jnp.bfloat16))
    return new_cache, attended, running
```

```python
import functools

import jax
import jax.numpy as jnp
from jax import lax
from jax.experimental import pallas as pl
from jax.experimental.pallas import tpu as pltpu
from jax.sharding import PartitionSpec as P

HEAD_DIM = 128
SINK = 4
REACH = 2
STEPS = 2
OFFSETS = tuple(o for o in range(-REACH, REACH + 1) if o != 0)
ORDER = (1, -1, 2, -2)
NEAR = (1, -1)
HEADER = 16
LANES = 128
STAY = 0
SENT = 1
POS = SENT + len(OFFSETS)
VMEM_LIMIT = 32 * 1024 * 1024

VMEM_SPEC = pl.BlockSpec(memory_space=pltpu.VMEM)
SMEM_SPEC = pl.BlockSpec(memory_space=pltpu.SMEM)
ANY_SPEC = pl.BlockSpec(memory_space=pl.ANY)
HBM_SPEC = pl.BlockSpec(memory_space=pltpu.HBM)


def shifted(block, distance):
    count = lax.axis_size("grp")
    return lax.ppermute(block, "grp", [(i, (i + distance) % count) for i in range(count)])


def relay_shifts(groups):
    known = {0, *(-o % groups for o in NEAR)}
    late = {-o % groups for o in OFFSETS}
    shifts = []
    while len(known | late) < groups:
        best = max(range(1, groups), key=lambda d: len(known | {(k - d) % groups for k in known} | late))
        known |= {(k - best) % groups for k in known}
        shifts.append(best)
    return shifts


def load_plan(sources, targets, sem):
    copies = [pltpu.make_async_copy(a, b, sem) for a, b in zip(sources, targets)]
    for copy in copies:
        copy.start()
    for copy in copies:
        copy.wait()


def row_iota(shape):
    return lax.broadcasted_iota(jnp.int32, shape, 0)


def lane_iota(shape):
    return lax.broadcasted_iota(jnp.int32, shape, len(shape) - 1)


def head_lanes(head):
    return slice(head * HEAD_DIM, (head + 1) * HEAD_DIM)


def block_rows(cache_len, head, side):
    return slice((2 * head + side) * cache_len, (2 * head + side + 1) * cache_len)


def pack_kernel(counts, hops_in, positions_in, kv, *refs):
    blocks, own = refs[: len(ORDER)], refs[len(ORDER)]
    hops, positions, plan_sem, sems = refs[len(ORDER) + 1 :]
    load_plan((hops_in, positions_in), (hops, positions), plan_sem)
    slots, _, cache_len, width = kv.shape
    live = counts[0]
    moves = [jnp.where(s < live, hops[s], 0) for s in range(slots)]
    picks, sents = {}, {}

    def pieces(k, pick):
        for head in range(width // HEAD_DIM):
            for side in range(2):
                yield pltpu.make_async_copy(
                    kv.at[pick, side, :, head_lanes(head)],
                    blocks[k].at[block_rows(cache_len, head, side)],
                    sems.at[k],
                )

    for k, offset in enumerate(ORDER):
        pick = jnp.int32(0)
        sent = jnp.int32(0)
        for s in range(slots):
            hit = moves[s] == offset
            pick = jnp.where(hit, s, pick)
            sent = jnp.where(hit, 1, sent)
        picks[offset], sents[offset] = pick, sent
        for piece in pieces(k, pick):
            piece.start()
    stay = jnp.int32(0)
    for s in range(slots):
        stay = stay + jnp.where((s < live) & (moves[s] == 0), 1, 0)
    shape = (HEADER, LANES)
    lane = lane_iota(shape)
    shared = jnp.where(lane == STAY, stay, 0)
    for k, offset in enumerate(OFFSETS):
        shared = jnp.where(lane == SENT + k, sents[offset], shared)
    own[...] = shared
    for k, offset in enumerate(ORDER):
        header = jnp.where(lane == POS, positions[picks[offset]], shared)
        blocks[k][-HEADER:, :] = header.astype(jnp.float32).astype(jnp.bfloat16)
    for k in range(len(ORDER)):
        for piece in pieces(k, 0):
            piece.wait()


def header_of(block):
    return block[-HEADER:, :].astype(jnp.float32).astype(jnp.int32)


def with_row(table, group, header):
    return jnp.where(row_iota(table.shape) == group, header[0:1], table)


def relay_kernel(own, *refs):
    blocks, table = refs[: len(NEAR)], refs[len(NEAR)]
    groups = table.shape[0]
    here = lax.axis_index("grp")
    rows = with_row(jnp.zeros(table.shape, jnp.int32), here, own[...])
    for offset, block in zip(NEAR, blocks):
        rows = with_row(rows, lax.rem(here - offset + groups, groups), header_of(block))
    table[...] = rows


def attend(load, keep, position, queries, fresh, store):
    width = fresh.shape[-1]
    group_size = queries.shape[-1] // width
    cache_len = load(0, 0).shape[0]
    window = cache_len - SINK
    first = SINK + lax.rem(position, window)
    second = SINK + lax.rem(position + 1, window)
    row = row_iota((cache_len, HEAD_DIM))
    score_shape = (group_size * STEPS, cache_len)
    stale = (row_iota(score_shape) % STEPS == 0) & (lane_iota(score_shape) == second)

    def updated(head, side):
        old = load(head, side)
        ones = [fresh[side, :, head_lanes(head)].astype(jnp.float32)[t : t + 1] for t in range(STEPS)]
        new = jnp.where(row == second, ones[1], jnp.where(row == first, ones[0], old.astype(jnp.float32)))
        new = new.astype(jnp.bfloat16)
        keep(head, side, new)
        return jnp.concatenate([new, old], axis=0)

    for head in range(width // HEAD_DIM):
        query = jnp.concatenate([queries[:, head_lanes(head * group_size + i)] for i in range(group_size)], axis=0)
        scores = lax.dot_general(
            query, updated(head, 0), (((1,), (1,)), ((), ())), preferred_element_type=jnp.float32
        )
        scores = jnp.where(stale, scores[:, cache_len:], scores[:, :cache_len]) * HEAD_DIM ** (-0.5)
        weights = jnp.exp(scores - jnp.max(scores, axis=1, keepdims=True))
        weights = weights / jnp.sum(weights, axis=1, keepdims=True)
        both = jnp.concatenate([jnp.where(stale, 0.0, weights), jnp.where(stale, weights, 0.0)], axis=1)
        mixed = jnp.dot(both.astype(jnp.bfloat16), updated(head, 1), preferred_element_type=jnp.float32)
        mixed = mixed.astype(jnp.bfloat16)
        for i in range(group_size):
            store(head * group_size + i, mixed[i * STEPS : (i + 1) * STEPS])


def stay_kernel(counts, hops_in, positions_in, kv, queries, fresh, cache, attended, *scratch):
    hops, positions, plan_sem, buffers, blank, order, load_sems, store_sem = scratch
    load_plan((hops_in, positions_in), (hops, positions), plan_sem)
    slots = kv.shape[0]
    live = counts[0]
    stay = jnp.int32(0)
    for s in range(slots):
        staying = (s < live) & (hops[s] == 0)

        @pl.when(staying)
        def _(s=s, stay=stay):
            order[stay] = s
            pltpu.make_async_copy(kv.at[s], buffers.at[stay], load_sems.at[stay]).start()

        stay = stay + jnp.where(staying, 1, 0)

    blank[...] = jnp.zeros_like(blank)

    def clear(j, carry):
        pltpu.make_async_copy(blank, cache.at[j], store_sem).start()
        attended[j] = jnp.zeros(attended.shape[1:], attended.dtype)
        return carry

    lax.fori_loop(stay, slots, clear, 0)

    def work(j, carry):
        pltpu.make_async_copy(kv.at[0], buffers.at[j], load_sems.at[j]).wait()

        def load(head, side):
            return buffers[j, side, :, head_lanes(head)]

        def keep(head, side, rows):
            buffers[j, side, :, head_lanes(head)] = rows

        def store(head, rows):
            attended[j, :, head_lanes(head)] = rows

        attend(load, keep, positions[order[j]], queries.at[j], fresh.at[j], store)
        pltpu.make_async_copy(buffers.at[j], cache.at[j], store_sem).start()
        return carry

    lax.fori_loop(0, stay, work, 0)

    def drain(j, carry):
        pltpu.make_async_copy(blank, cache.at[0], store_sem).wait()
        return carry

    lax.fori_loop(0, slots, drain, 0)


def arrive_kernel(own, table, queries, fresh, cache_in, attended_in, *refs):
    blocks = refs[: len(ORDER)]
    cache, attended, served, rows, rows_smem, buffers, heads, rows_sem, store_sems = refs[len(ORDER) :]
    del cache_in, attended_in
    groups = table.shape[0]
    cache_len = cache.shape[2]
    here = lax.axis_index("grp")
    headers = {offset: header_of(block) for offset, block in zip(ORDER, blocks)}
    everyone = table[...]
    for offset in ORDER:
        if offset not in NEAR:
            everyone = with_row(everyone, lax.rem(here - offset + groups, groups), headers[offset])
    rows[...] = everyone
    rows_copy = pltpu.make_async_copy(rows, rows_smem, rows_sem)
    rows_copy.start()

    def entry(header, lane):
        shape = header[0:1].shape
        return jnp.sum(jnp.where(lane_iota(shape) == lane, header[0:1], 0))

    places = {}
    place = entry(own[...], STAY)
    for k, offset in enumerate(OFFSETS):
        present = entry(headers[offset], SENT + k) > 0
        places[offset] = (present, place)
        place = place + jnp.where(present, 1, 0)

    def stores(i, slot):
        return (
            pltpu.make_async_copy(buffers.at[i], cache.at[slot], store_sems.at[i, 0]),
            pltpu.make_async_copy(heads.at[i], attended.at[slot], store_sems.at[i, 1]),
        )

    for i, offset in enumerate(ORDER):
        present, slot = places[offset]

        @pl.when(present)
        def _(i=i, slot=slot, offset=offset):
            def load(head, side):
                return blocks[i][block_rows(cache_len, head, side), :]

            def keep(head, side, rows):
                buffers[i, side, :, head_lanes(head)] = rows

            def store(head, rows):
                heads[i, :, head_lanes(head)] = rows

            attend(load, keep, entry(headers[offset], POS), queries.at[slot], fresh.at[slot], store)
            for copy in stores(i, slot):
                copy.start()

    rows_copy.wait()

    def count(g, carry):
        total = rows_smem[g, STAY]
        for k, offset in enumerate(OFFSETS):
            total = total + rows_smem[lax.rem(g - offset + groups, groups), SENT + k]
        served[g] = total
        return carry

    lax.fori_loop(0, groups, count, 0)

    for i, offset in enumerate(ORDER):
        present, slot = places[offset]

        @pl.when(present)
        def _(i=i, slot=slot):
            for copy in stores(i, slot):
                copy.wait()


def per_device(counts, hop_offsets, write_pos, kv_cache, queries, fresh_kv):
    groups = lax.axis_size("grp")
    slots = kv_cache.shape[0]
    stream = kv_cache.shape[1:]
    cache_len, width = stream[1:]
    head_row = queries.shape[1:]
    params = pltpu.CompilerParams(vmem_limit_bytes=VMEM_LIMIT)
    plan = [counts, *(pltpu.with_memory_space_constraint(a, pltpu.HBM) for a in (hop_offsets, write_pos, kv_cache))]
    plan_scratch = [
        pltpu.SMEM(hop_offsets.shape, jnp.int32),
        pltpu.SMEM(write_pos.shape, jnp.int32),
        pltpu.SemaphoreType.DMA,
    ]
    block = jax.ShapeDtypeStruct((width // HEAD_DIM * 2 * cache_len + HEADER, HEAD_DIM), kv_cache.dtype)
    table = jax.ShapeDtypeStruct((groups, LANES), jnp.int32)
    cache = jax.ShapeDtypeStruct(kv_cache.shape, kv_cache.dtype)
    heads = jax.ShapeDtypeStruct(queries.shape, queries.dtype)
    *blocks, own = pl.pallas_call(
        pack_kernel,
        out_shape=[block] * len(ORDER) + [jax.ShapeDtypeStruct((HEADER, LANES), jnp.int32)],
        in_specs=[SMEM_SPEC] + [HBM_SPEC] * 3,
        out_specs=[VMEM_SPEC] * (len(ORDER) + 1),
        scratch_shapes=plan_scratch + [pltpu.SemaphoreType.DMA((len(ORDER),))],
        compiler_params=params,
        name="pack",
    )(*plan)
    arrived = {offset: shifted(block, offset) for offset, block in zip(ORDER, blocks)}

    new_cache, attended = pl.pallas_call(
        stay_kernel,
        out_shape=[cache, heads],
        in_specs=[SMEM_SPEC] + [HBM_SPEC] * 3 + [VMEM_SPEC, VMEM_SPEC],
        out_specs=[ANY_SPEC, VMEM_SPEC],
        scratch_shapes=plan_scratch
        + [
            pltpu.VMEM(kv_cache.shape, kv_cache.dtype),
            pltpu.VMEM(stream, kv_cache.dtype),
            pltpu.SMEM((slots,), jnp.int32),
            pltpu.SemaphoreType.DMA((slots,)),
            pltpu.SemaphoreType.DMA,
        ],
        compiler_params=params,
        cost_estimate=pl.CostEstimate(flops=50_000_000, bytes_accessed=4 * kv_cache.size, transcendentals=0),
        name="stay",
    )(*plan, queries, fresh_kv)

    known = pl.pallas_call(
        relay_kernel,
        out_shape=table,
        in_specs=[VMEM_SPEC] * (1 + len(NEAR)),
        out_specs=VMEM_SPEC,
        compiler_params=params,
        name="relay",
    )(own, *[arrived[offset] for offset in NEAR])
    for distance in relay_shifts(groups):
        known = jnp.maximum(known, shifted(known, distance))

    return pl.pallas_call(
        arrive_kernel,
        out_shape=[cache, heads, jax.ShapeDtypeStruct((groups,), jnp.int32)],
        in_specs=[VMEM_SPEC] * 4 + [ANY_SPEC] * 2 + [VMEM_SPEC] * len(ORDER),
        out_specs=[ANY_SPEC, ANY_SPEC, SMEM_SPEC],
        scratch_shapes=[
            pltpu.VMEM(table.shape, jnp.int32),
            pltpu.SMEM(table.shape, jnp.int32),
            pltpu.VMEM((len(ORDER),) + stream, kv_cache.dtype),
            pltpu.VMEM((len(ORDER),) + head_row, queries.dtype),
            pltpu.SemaphoreType.DMA,
            pltpu.SemaphoreType.DMA((len(ORDER), 2)),
        ],
        input_output_aliases={4: 0, 5: 1},
        compiler_params=params,
        name="arrive",
    )(own, known, queries, fresh_kv, new_cache, attended, *[arrived[offset] for offset in ORDER])


def solution(mesh):
    return jax.shard_map(
        per_device,
        mesh=mesh,
        in_specs=(
            P(("rep", "grp")),
            P(("rep", "grp")),
            P(("rep", "grp")),
            P(("rep", "grp"), None, None, "tp"),
            P(("rep", "grp"), None, "tp"),
            P(("rep", "grp"), None, None, "tp"),
        ),
        out_specs=(P(("rep", "grp"), None, None, "tp"), P(("rep", "grp"), None, "tp"), P("rep")),
        check_vma=False,
    )
```

```python
import functools

import jax
import jax.numpy as jnp
from jax import lax
from jax.experimental import pallas as pl
from jax.experimental.pallas import tpu as pltpu
from jax.sharding import PartitionSpec as P

HEAD_DIM = 128
SINK = 4
REACH = 2
STEPS = 2
OFFSETS = tuple(o for o in range(-REACH, REACH + 1) if o != 0)
ORDER = (-2, -1, 1, 2)
NEAR = (-1, -2)
ARRIVALS = ((-2, -1, 1), (2,))
PATCH = 16
LANES = HEAD_DIM
STAY = 0
SENT = 1
POS = SENT + len(OFFSETS)
VMEM_LIMIT = 32 * 1024 * 1024

VMEM_SPEC = pl.BlockSpec(memory_space=pltpu.VMEM)
SMEM_SPEC = pl.BlockSpec(memory_space=pltpu.SMEM)
ANY_SPEC = pl.BlockSpec(memory_space=pl.ANY)
HBM_SPEC = pl.BlockSpec(memory_space=pltpu.HBM)


def shifted(block, distance):
    count = lax.axis_size("grp")
    return lax.ppermute(block, "grp", [(i, (i + distance) % count) for i in range(count)])


def relay_shifts(groups):
    known = {0, *(-o % groups for o in NEAR)}
    late = {-o % groups for o in OFFSETS}
    shifts = []
    while len(known | late) < groups:
        best = max(range(1, groups), key=lambda d: len(known | {(k - d) % groups for k in known} | late))
        known |= {(k - best) % groups for k in known}
        shifts.append(best)
    return shifts


def load_plan(sources, targets, sem):
    copies = [pltpu.make_async_copy(a, b, sem) for a, b in zip(sources, targets)]
    for copy in copies:
        copy.start()
    for copy in copies:
        copy.wait()


def row_iota(shape):
    return lax.broadcasted_iota(jnp.int32, shape, 0)


def lane_iota(shape):
    return lax.broadcasted_iota(jnp.int32, shape, len(shape) - 1)


def head_lanes(head):
    return slice(head * HEAD_DIM, (head + 1) * HEAD_DIM)


def first_written(position, cache_len):
    return SINK + lax.rem(position, cache_len - SINK)


def pack_kernel(counts, hops_in, positions_in, kv, *refs):
    blocks = refs[: len(ORDER)]
    hops, positions, plan_sem, sems = refs[len(ORDER) :]
    load_plan((hops_in, positions_in), (hops, positions), plan_sem)
    slots, _, cache_len, _ = kv.shape
    live = counts[0]
    moves = [jnp.where(s < live, hops[s], 0) for s in range(slots)]
    picks, sents = {}, {}

    copies = []
    for k, offset in enumerate(ORDER):
        pick = jnp.int32(0)
        sent = jnp.int32(0)
        for s in range(slots):
            hit = moves[s] == offset
            pick = jnp.where(hit, s, pick)
            sent = jnp.where(hit, 1, sent)
        picks[offset], sents[offset] = pick, sent
        copies.append(pltpu.make_async_copy(kv.at[pick], blocks[k], sems.at[k]))
        copies[k].start()
    stay = jnp.int32(0)
    for s in range(slots):
        stay = stay + jnp.where((s < live) & (moves[s] == 0), 1, 0)
    shape = (PATCH, LANES)
    lane, row = lane_iota(shape), row_iota(shape)
    shared = jnp.where(lane == STAY, stay, 0)
    for k, offset in enumerate(OFFSETS):
        shared = jnp.where(lane == SENT + k, sents[offset], shared)
    for k, offset in enumerate(ORDER):
        position = positions[picks[offset]]
        header = jnp.where(lane == POS, position, shared).astype(jnp.float32)
        first = first_written(position, cache_len)
        base = pl.multiple_of((first // PATCH) * PATCH, PATCH)
        copies[k].wait()
        top = blocks[k][0, :PATCH, :LANES].astype(jnp.float32)
        blocks[k][0, :PATCH, :LANES] = jnp.where(row == 0, header, top).astype(jnp.bfloat16)
        patch = blocks[k][0, pl.ds(base, PATCH), :LANES].astype(jnp.float32)
        patch = jnp.where(row == first - base, top[0:1], patch)
        blocks[k][0, pl.ds(base, PATCH), :LANES] = patch.astype(jnp.bfloat16)


def header_of(block):
    return block[0, :PATCH, :LANES].astype(jnp.float32).astype(jnp.int32)


def with_row(table, group, header):
    return jnp.where(row_iota(table.shape) == group, header[0:1], table)


def relay_kernel(own, *refs):
    blocks, table = refs[: len(NEAR)], refs[len(NEAR)]
    groups = table.shape[0]
    here = lax.axis_index("grp")
    rows = with_row(jnp.zeros(table.shape, jnp.int32), here, own[...])
    for offset, block in zip(NEAR, blocks):
        rows = with_row(rows, lax.rem(here - offset + groups, groups), header_of(block))
    table[...] = rows


def attend(old, new, has_header, position, queries, fresh, heads, flush):
    cache_len, width = old.shape[1:]
    head_count = width // HEAD_DIM
    group_size = queries.shape[-1] // width
    first = first_written(position, cache_len)
    second = first_written(position + 1, cache_len)
    for side in range(2):
        written = fresh[side].astype(jnp.float32)
        for head in range(head_count):
            lanes = head_lanes(head)
            rows = old[side, :, lanes].astype(jnp.float32)
            row = row_iota(rows.shape)
            if has_header and (side, head) == (0, 0):
                top = jnp.sum(jnp.where(row == first, rows, 0.0), axis=0, keepdims=True)
                rows = jnp.where(row == 0, top, rows)
            rows = jnp.where(row == second, written[1:2, lanes], jnp.where(row == first, written[0:1, lanes], rows))
            new[side, :, lanes] = rows.astype(jnp.bfloat16)
    flush()

    def both(side, head):
        return jnp.concatenate([new[side, :, head_lanes(head)], old[side, :, head_lanes(head)]], axis=0)

    scores = []
    for head in range(head_count):
        query = jnp.concatenate([queries[:, head_lanes(head * group_size + i)] for i in range(group_size)], axis=0)
        scores.append(
            lax.dot_general(query, both(0, head), (((1,), (1,)), ((), ())), preferred_element_type=jnp.float32)
        )
    scores = jnp.concatenate(scores, axis=0)
    shape = (scores.shape[0], cache_len)
    stale = (row_iota(shape) % STEPS == 0) & (lane_iota(shape) == second)
    scores = jnp.where(stale, scores[:, cache_len:], scores[:, :cache_len]) * HEAD_DIM ** (-0.5)
    weights = jnp.exp(scores - jnp.max(scores, axis=1, keepdims=True))
    weights = weights / jnp.sum(weights, axis=1, keepdims=True)
    weights = jnp.concatenate([jnp.where(stale, 0.0, weights), jnp.where(stale, weights, 0.0)], axis=1)
    weights = weights.astype(jnp.bfloat16)
    for head in range(head_count):
        rows = slice(head * group_size * STEPS, (head + 1) * group_size * STEPS)
        mixed = jnp.dot(weights[rows], both(1, head), preferred_element_type=jnp.float32).astype(jnp.bfloat16)
        for i in range(group_size):
            heads[:, head_lanes(head * group_size + i)] = mixed[i * STEPS : (i + 1) * STEPS]


def stay_kernel(counts, hops_in, positions_in, kv, queries, fresh, cache, attended, own, *scratch):
    hops, positions, plan_sem, buffers, updated, blank, order, load_sems, store_sem = scratch
    load_plan((hops_in, positions_in), (hops, positions), plan_sem)
    slots = kv.shape[0]
    live = counts[0]
    stay = jnp.int32(0)
    for s in range(slots):
        staying = (s < live) & (hops[s] == 0)

        @pl.when(staying)
        def _(s=s, stay=stay):
            order[stay] = s
            pltpu.make_async_copy(kv.at[s], buffers.at[stay], load_sems.at[stay]).start()

        stay = stay + jnp.where(staying, 1, 0)

    shape = own.shape
    row = jnp.where(lane_iota(shape) == STAY, stay, 0)
    for k, offset in enumerate(OFFSETS):
        sent = jnp.int32(0)
        for s in range(slots):
            sent = jnp.where((s < live) & (hops[s] == offset), 1, sent)
        row = jnp.where(lane_iota(shape) == SENT + k, sent, row)
    own[...] = row
    blank[...] = jnp.zeros_like(blank)

    def clear(j, carry):
        pltpu.make_async_copy(blank, cache.at[j], store_sem).start()
        attended[j] = jnp.zeros(attended.shape[1:], attended.dtype)
        return carry

    lax.fori_loop(stay, slots, clear, 0)

    def work(j, carry):
        pltpu.make_async_copy(kv.at[0], buffers.at[j], load_sems.at[j]).wait()

        def flush():
            pltpu.make_async_copy(updated.at[j], cache.at[j], store_sem).start()

        attend(
            buffers.at[j], updated.at[j], False, positions[order[j]], queries.at[j], fresh.at[j], attended.at[j], flush
        )
        return carry

    lax.fori_loop(0, stay, work, 0)

    def drain(j, carry):
        pltpu.make_async_copy(blank, cache.at[0], store_sem).wait()
        return carry

    lax.fori_loop(0, slots, drain, 0)


def arrive_kernel(mine, last, own, queries, fresh, cache_in, attended_in, *refs):
    del cache_in, attended_in
    seen = OFFSETS[: OFFSETS.index(mine[-1]) + 1]
    blocks, refs = dict(zip(seen, refs)), refs[len(seen) :]
    if last:
        known, cache, attended, served, buffers, heads, store_sems = refs
    else:
        cache, attended, buffers, heads, store_sems = refs
    headers = {offset: header_of(block) for offset, block in blocks.items()}

    def entry(header, lane):
        shape = header[0:1].shape
        return jnp.sum(jnp.where(lane_iota(shape) == lane, header[0:1], 0))

    places = {}
    place = entry(own[...], STAY)
    for k, offset in enumerate(seen):
        present = entry(headers[offset], SENT + k) > 0
        places[offset] = (present, place)
        place = place + jnp.where(present, 1, 0)

    def stores(i, slot):
        return (
            pltpu.make_async_copy(buffers.at[i], cache.at[slot], store_sems.at[i, 0]),
            pltpu.make_async_copy(heads.at[i], attended.at[slot], store_sems.at[i, 1]),
        )

    for i, offset in enumerate(mine):
        present, slot = places[offset]

        @pl.when(present)
        def _(i=i, slot=slot, offset=offset):
            into_cache, into_attended = stores(i, slot)
            position = entry(headers[offset], POS)
            attend(
                blocks[offset],
                buffers.at[i],
                True,
                position,
                queries.at[slot],
                fresh.at[slot],
                heads.at[i],
                into_cache.start,
            )
            into_attended.start()

    if last:
        groups = known.shape[0]
        here = lax.axis_index("grp")
        rows = known[...]
        for offset in OFFSETS:
            rows = with_row(rows, lax.rem(here - offset + groups, groups), headers[offset])
        served[...] = count_served(rows)

    for i, offset in enumerate(mine):
        present, slot = places[offset]

        @pl.when(present)
        def _(i=i, slot=slot):
            for copy in stores(i, slot):
                copy.wait()


def count_served(rows):
    groups = rows.shape[0]

    def column(lane, shift):
        moved = pltpu.roll(rows, shift % groups, 0) if shift % groups else rows
        return jnp.sum(jnp.where(lane_iota(rows.shape) == lane, moved, 0), axis=1, keepdims=True)

    total = column(STAY, 0)
    for k, offset in enumerate(OFFSETS):
        total = total + column(SENT + k, offset)
    square = (groups, groups)
    return jnp.sum(jnp.where(row_iota(square) == lane_iota(square), total, 0), axis=0)


def per_device(counts, hop_offsets, write_pos, kv_cache, queries, fresh_kv):
    groups = lax.axis_size("grp")
    slots = kv_cache.shape[0]
    stream = kv_cache.shape[1:]
    head_row = queries.shape[1:]
    params = pltpu.CompilerParams(vmem_limit_bytes=VMEM_LIMIT)
    plan = [counts, *(pltpu.with_memory_space_constraint(a, pltpu.HBM) for a in (hop_offsets, write_pos, kv_cache))]
    plan_scratch = [
        pltpu.SMEM(hop_offsets.shape, jnp.int32),
        pltpu.SMEM(write_pos.shape, jnp.int32),
        pltpu.SemaphoreType.DMA,
    ]
    block = jax.ShapeDtypeStruct(stream, kv_cache.dtype)
    table = jax.ShapeDtypeStruct((groups, LANES), jnp.int32)
    cache = jax.ShapeDtypeStruct(kv_cache.shape, kv_cache.dtype)
    heads = jax.ShapeDtypeStruct(queries.shape, queries.dtype)
    blocks = pl.pallas_call(
        pack_kernel,
        out_shape=[block] * len(ORDER),
        in_specs=[SMEM_SPEC] + [HBM_SPEC] * 3,
        out_specs=[VMEM_SPEC] * len(ORDER),
        scratch_shapes=plan_scratch + [pltpu.SemaphoreType.DMA((len(ORDER),))],
        compiler_params=params,
        name="pack",
    )(*plan)
    arrived = {offset: shifted(block, offset) for offset, block in zip(ORDER, blocks)}

    new_cache, attended, own = pl.pallas_call(
        stay_kernel,
        out_shape=[cache, heads, jax.ShapeDtypeStruct((1, LANES), jnp.int32)],
        in_specs=[SMEM_SPEC] + [HBM_SPEC] * 3 + [VMEM_SPEC, VMEM_SPEC],
        out_specs=[ANY_SPEC, VMEM_SPEC, VMEM_SPEC],
        scratch_shapes=plan_scratch
        + [
            pltpu.VMEM(kv_cache.shape, kv_cache.dtype),
            pltpu.VMEM(kv_cache.shape, kv_cache.dtype),
            pltpu.VMEM(stream, kv_cache.dtype),
            pltpu.SMEM((slots,), jnp.int32),
            pltpu.SemaphoreType.DMA((slots,)),
            pltpu.SemaphoreType.DMA,
        ],
        compiler_params=params,
        cost_estimate=pl.CostEstimate(flops=50_000_000, bytes_accessed=4 * kv_cache.size, transcendentals=0),
        name="stay",
    )(*plan, queries, fresh_kv)

    known = pl.pallas_call(
        relay_kernel,
        out_shape=table,
        in_specs=[VMEM_SPEC] * (1 + len(NEAR)),
        out_specs=VMEM_SPEC,
        compiler_params=params,
        name="relay",
    )(own, *[arrived[offset] for offset in NEAR])
    for distance in relay_shifts(groups):
        known = jnp.maximum(known, shifted(known, distance))

    for mine in ARRIVALS:
        last = mine[-1] == OFFSETS[-1]
        new_cache, attended, *served = pl.pallas_call(
            functools.partial(arrive_kernel, mine, last),
            out_shape=[cache, heads] + [jax.ShapeDtypeStruct((groups,), jnp.int32)] * last,
            in_specs=[VMEM_SPEC] * 3 + [ANY_SPEC] * 2 + [VMEM_SPEC] * (OFFSETS.index(mine[-1]) + 1 + last),
            out_specs=[ANY_SPEC] * 2 + [VMEM_SPEC] * last,
            scratch_shapes=[
                pltpu.VMEM((len(mine),) + stream, kv_cache.dtype),
                pltpu.VMEM((len(mine),) + head_row, queries.dtype),
                pltpu.SemaphoreType.DMA((len(mine), 2)),
            ],
            input_output_aliases={3: 0, 4: 1},
            compiler_params=params,
            name="arrive",
        )(
            own,
            queries,
            fresh_kv,
            new_cache,
            attended,
            *[arrived[offset] for offset in OFFSETS if offset <= mine[-1]],
            *[known] * last,
        )
    return (new_cache, attended, served[0])


def solution(mesh):
    return jax.shard_map(
        per_device,
        mesh=mesh,
        in_specs=(
            P(("rep", "grp")),
            P(("rep", "grp")),
            P(("rep", "grp")),
            P(("rep", "grp"), None, None, "tp"),
            P(("rep", "grp"), None, "tp"),
            P(("rep", "grp"), None, None, "tp"),
        ),
        out_specs=(P(("rep", "grp"), None, None, "tp"), P(("rep", "grp"), None, "tp"), P("rep")),
        check_vma=False,
    )
```

```python
import functools

import jax
import jax.numpy as jnp
from jax import lax
from jax.experimental import pallas as pl
from jax.experimental.pallas import tpu as pltpu
from jax.sharding import PartitionSpec as P

HEAD_DIM = 128
SINK = 4
REACH = 2
STEPS = 2
OFFSETS = tuple(o for o in range(-REACH, REACH + 1) if o != 0)
PACKS = ((-2, -1), (1, 2))
NEAR = (-1, -2)
ARRIVALS = ((-2, -1, 1), (2,))
PATCH = 16
LANES = HEAD_DIM
STAY = 0
SENT = 1
POS = SENT + len(OFFSETS)
VMEM_LIMIT = 32 * 1024 * 1024

VMEM_SPEC = pl.BlockSpec(memory_space=pltpu.VMEM)
SMEM_SPEC = pl.BlockSpec(memory_space=pltpu.SMEM)
ANY_SPEC = pl.BlockSpec(memory_space=pl.ANY)
HBM_SPEC = pl.BlockSpec(memory_space=pltpu.HBM)


def shifted(block, distance):
    count = lax.axis_size("grp")
    return lax.ppermute(block, "grp", [(i, (i + distance) % count) for i in range(count)])


def relay_shifts(groups):
    known = {0, *(-o % groups for o in NEAR)}
    late = {-o % groups for o in OFFSETS}
    shifts = []
    while len(known | late) < groups:
        best = max(range(1, groups), key=lambda d: len(known | {(k - d) % groups for k in known} | late))
        known |= {(k - best) % groups for k in known}
        shifts.append(best)
    return shifts


def load_plan(sources, targets, sem):
    copies = [pltpu.make_async_copy(a, b, sem) for a, b in zip(sources, targets)]
    for copy in copies:
        copy.start()
    for copy in copies:
        copy.wait()


def row_iota(shape):
    return lax.broadcasted_iota(jnp.int32, shape, 0)


def lane_iota(shape):
    return lax.broadcasted_iota(jnp.int32, shape, len(shape) - 1)


def head_lanes(head):
    return slice(head * HEAD_DIM, (head + 1) * HEAD_DIM)


def first_written(position, cache_len):
    return SINK + lax.rem(position, cache_len - SINK)


def plan_row(hops, live, slots, shape):
    lane = lane_iota(shape)
    stay = jnp.int32(0)
    for s in range(slots):
        stay = stay + jnp.where((s < live) & (hops[s] == 0), 1, 0)
    values = jnp.where(lane == STAY, stay, 0)
    for k, offset in enumerate(OFFSETS):
        sent = jnp.int32(0)
        for s in range(slots):
            sent = jnp.where((s < live) & (hops[s] == offset), 1, sent)
        values = jnp.where(lane == SENT + k, sent, values)
    return values


def pack_kernel(offsets, counts, hops_in, positions_in, kv, *refs):
    blocks = refs[: len(offsets)]
    hops, positions, plan_sem, sems = refs[len(offsets) :]
    load_plan((hops_in, positions_in), (hops, positions), plan_sem)
    slots, _, cache_len, _ = kv.shape
    picks, copies = [], []
    for k, offset in enumerate(offsets):
        pick = jnp.int32(0)
        for s in range(slots):
            pick = jnp.where(hops[s] == offset, s, pick)
        picks.append(pick)
        copies.append(pltpu.make_async_copy(kv.at[pick], blocks[k], sems.at[k]))
        copies[k].start()
    shape = (PATCH, LANES)
    lane, row = lane_iota(shape), row_iota(shape)
    shared = plan_row(hops, counts[0], slots, shape)
    for k in range(len(offsets)):
        position = positions[picks[k]]
        header = jnp.where(lane == POS, position, shared).astype(jnp.float32)
        first = first_written(position, cache_len)
        base = pl.multiple_of((first // PATCH) * PATCH, PATCH)
        copies[k].wait()
        top = blocks[k][0, :PATCH, :LANES].astype(jnp.float32)
        blocks[k][0, :PATCH, :LANES] = jnp.where(row == 0, header, top).astype(jnp.bfloat16)
        patch = blocks[k][0, pl.ds(base, PATCH), :LANES].astype(jnp.float32)
        patch = jnp.where(row == first - base, top[0:1], patch)
        blocks[k][0, pl.ds(base, PATCH), :LANES] = patch.astype(jnp.bfloat16)


def header_of(block):
    return block[0, :PATCH, :LANES].astype(jnp.float32).astype(jnp.int32)


def with_row(table, group, header):
    return jnp.where(row_iota(table.shape) == group, header[0:1], table)


def relay_kernel(own, *refs):
    blocks, table = refs[: len(NEAR)], refs[len(NEAR)]
    groups = table.shape[0]
    here = lax.axis_index("grp")
    rows = with_row(jnp.zeros(table.shape, jnp.int32), here, own[...])
    for offset, block in zip(NEAR, blocks):
        rows = with_row(rows, lax.rem(here - offset + groups, groups), header_of(block))
    table[...] = rows


def attend(old, new, has_header, position, queries, fresh, heads, flush):
    cache_len, width = old.shape[1:]
    head_count = width // HEAD_DIM
    group_size = queries.shape[-1] // width
    first = first_written(position, cache_len)
    second = first_written(position + 1, cache_len)
    for side in range(2):
        written = fresh[side].astype(jnp.float32)
        for head in range(head_count):
            lanes = head_lanes(head)
            rows = old[side, :, lanes].astype(jnp.float32)
            row = row_iota(rows.shape)
            if has_header and (side, head) == (0, 0):
                top = jnp.sum(jnp.where(row == first, rows, 0.0), axis=0, keepdims=True)
                rows = jnp.where(row == 0, top, rows)
            rows = jnp.where(row == second, written[1:2, lanes], jnp.where(row == first, written[0:1, lanes], rows))
            new[side, :, lanes] = rows.astype(jnp.bfloat16)
    flush()

    def both(side, head):
        return jnp.concatenate([new[side, :, head_lanes(head)], old[side, :, head_lanes(head)]], axis=0)

    scores = []
    for head in range(head_count):
        query = jnp.concatenate([queries[:, head_lanes(head * group_size + i)] for i in range(group_size)], axis=0)
        scores.append(
            lax.dot_general(query, both(0, head), (((1,), (1,)), ((), ())), preferred_element_type=jnp.float32)
        )
    scores = jnp.concatenate(scores, axis=0)
    shape = (scores.shape[0], cache_len)
    stale = (row_iota(shape) % STEPS == 0) & (lane_iota(shape) == second)
    scores = jnp.where(stale, scores[:, cache_len:], scores[:, :cache_len]) * HEAD_DIM ** (-0.5)
    weights = jnp.exp(scores - jnp.max(scores, axis=1, keepdims=True))
    weights = weights / jnp.sum(weights, axis=1, keepdims=True)
    weights = jnp.concatenate([jnp.where(stale, 0.0, weights), jnp.where(stale, weights, 0.0)], axis=1)
    weights = weights.astype(jnp.bfloat16)
    for head in range(head_count):
        rows = slice(head * group_size * STEPS, (head + 1) * group_size * STEPS)
        mixed = jnp.dot(weights[rows], both(1, head), preferred_element_type=jnp.float32).astype(jnp.bfloat16)
        for i in range(group_size):
            heads[:, head_lanes(head * group_size + i)] = mixed[i * STEPS : (i + 1) * STEPS]


def stay_kernel(counts, hops_in, positions_in, kv, queries, fresh, cache, attended, own, *scratch):
    hops, positions, plan_sem, buffers, updated, blank, order, load_sems, store_sem = scratch
    load_plan((hops_in, positions_in), (hops, positions), plan_sem)
    slots = kv.shape[0]
    live = counts[0]
    stay = jnp.int32(0)
    for s in range(slots):
        staying = (s < live) & (hops[s] == 0)

        @pl.when(staying)
        def _(s=s, stay=stay):
            order[stay] = s
            pltpu.make_async_copy(kv.at[s], buffers.at[stay], load_sems.at[stay]).start()

        stay = stay + jnp.where(staying, 1, 0)

    own[...] = plan_row(hops, live, slots, own.shape)
    blank[...] = jnp.zeros_like(blank)

    def clear(j, carry):
        pltpu.make_async_copy(blank, cache.at[j], store_sem).start()
        attended[j] = jnp.zeros(attended.shape[1:], attended.dtype)
        return carry

    lax.fori_loop(stay, slots, clear, 0)

    def work(j, carry):
        pltpu.make_async_copy(kv.at[0], buffers.at[j], load_sems.at[j]).wait()

        def flush():
            pltpu.make_async_copy(updated.at[j], cache.at[j], store_sem).start()

        attend(
            buffers.at[j], updated.at[j], False, positions[order[j]], queries.at[j], fresh.at[j], attended.at[j], flush
        )
        return carry

    lax.fori_loop(0, stay, work, 0)

    def drain(j, carry):
        pltpu.make_async_copy(blank, cache.at[0], store_sem).wait()
        return carry

    lax.fori_loop(0, slots, drain, 0)


def arrive_kernel(mine, last, own, queries, fresh, cache_in, attended_in, *refs):
    del cache_in, attended_in
    seen = OFFSETS[: OFFSETS.index(mine[-1]) + 1]
    blocks, refs = dict(zip(seen, refs)), refs[len(seen) :]
    if last:
        known, cache, attended, served, buffers, heads, store_sems, total, total_sem = refs
    else:
        cache, attended, buffers, heads, store_sems = refs
    headers = {offset: header_of(block) for offset, block in blocks.items()}

    def entry(header, lane):
        shape = header[0:1].shape
        return jnp.sum(jnp.where(lane_iota(shape) == lane, header[0:1], 0))

    places = {}
    place = entry(own[...], STAY)
    for k, offset in enumerate(seen):
        present = entry(headers[offset], SENT + k) > 0
        places[offset] = (present, place)
        place = place + jnp.where(present, 1, 0)

    def stores(i, slot):
        return (
            pltpu.make_async_copy(buffers.at[i], cache.at[slot], store_sems.at[i, 0]),
            pltpu.make_async_copy(heads.at[i], attended.at[slot], store_sems.at[i, 1]),
        )

    for i, offset in enumerate(mine):
        present, slot = places[offset]

        @pl.when(present)
        def _(i=i, slot=slot, offset=offset):
            into_cache, into_attended = stores(i, slot)
            position = entry(headers[offset], POS)
            attend(
                blocks[offset],
                buffers.at[i],
                True,
                position,
                queries.at[slot],
                fresh.at[slot],
                heads.at[i],
                into_cache.start,
            )
            into_attended.start()

    if last:
        groups = known.shape[0]
        here = lax.axis_index("grp")
        rows = known[...]
        for offset in OFFSETS:
            rows = with_row(rows, lax.rem(here - offset + groups, groups), headers[offset])
        total[...] = count_served(rows)
        into_served = pltpu.make_async_copy(total, served, total_sem)
        into_served.start()

    for i, offset in enumerate(mine):
        present, slot = places[offset]

        @pl.when(present)
        def _(i=i, slot=slot):
            for copy in stores(i, slot):
                copy.wait()

    if last:
        into_served.wait()


def count_served(rows):
    groups = rows.shape[0]

    def column(lane, shift):
        moved = pltpu.roll(rows, shift % groups, 0) if shift % groups else rows
        return jnp.sum(jnp.where(lane_iota(rows.shape) == lane, moved, 0), axis=1, keepdims=True)

    total = column(STAY, 0)
    for k, offset in enumerate(OFFSETS):
        total = total + column(SENT + k, offset)
    square = (groups, groups)
    return jnp.sum(jnp.where(row_iota(square) == lane_iota(square), total, 0), axis=0)


def per_device(counts, hop_offsets, write_pos, kv_cache, queries, fresh_kv):
    groups = lax.axis_size("grp")
    slots = kv_cache.shape[0]
    stream = kv_cache.shape[1:]
    head_row = queries.shape[1:]
    params = pltpu.CompilerParams(vmem_limit_bytes=VMEM_LIMIT)
    plan = [counts, *(pltpu.with_memory_space_constraint(a, pltpu.HBM) for a in (hop_offsets, write_pos, kv_cache))]
    plan_scratch = [
        pltpu.SMEM(hop_offsets.shape, jnp.int32),
        pltpu.SMEM(write_pos.shape, jnp.int32),
        pltpu.SemaphoreType.DMA,
    ]
    block = jax.ShapeDtypeStruct(stream, kv_cache.dtype)
    table = jax.ShapeDtypeStruct((groups, LANES), jnp.int32)
    cache = jax.ShapeDtypeStruct(kv_cache.shape, kv_cache.dtype)
    heads = jax.ShapeDtypeStruct(queries.shape, queries.dtype)
    arrived = {}
    for offsets in PACKS:
        blocks = pl.pallas_call(
            functools.partial(pack_kernel, offsets),
            out_shape=[block] * len(offsets),
            in_specs=[SMEM_SPEC] + [HBM_SPEC] * 3,
            out_specs=[VMEM_SPEC] * len(offsets),
            scratch_shapes=plan_scratch + [pltpu.SemaphoreType.DMA((len(offsets),))],
            compiler_params=params,
            name="pack",
        )(*plan)
        for offset, outgoing in zip(offsets, blocks):
            arrived[offset] = shifted(outgoing, offset)

    new_cache, attended, own = pl.pallas_call(
        stay_kernel,
        out_shape=[cache, heads, jax.ShapeDtypeStruct((1, LANES), jnp.int32)],
        in_specs=[SMEM_SPEC] + [HBM_SPEC] * 3 + [VMEM_SPEC, VMEM_SPEC],
        out_specs=[ANY_SPEC, VMEM_SPEC, VMEM_SPEC],
        scratch_shapes=plan_scratch
        + [
            pltpu.VMEM(kv_cache.shape, kv_cache.dtype),
            pltpu.VMEM(kv_cache.shape, kv_cache.dtype),
            pltpu.VMEM(stream, kv_cache.dtype),
            pltpu.SMEM((slots,), jnp.int32),
            pltpu.SemaphoreType.DMA((slots,)),
            pltpu.SemaphoreType.DMA,
        ],
        compiler_params=params,
        cost_estimate=pl.CostEstimate(flops=50_000_000, bytes_accessed=4 * kv_cache.size, transcendentals=0),
        name="stay",
    )(*plan, queries, fresh_kv)

    known = pl.pallas_call(
        relay_kernel,
        out_shape=table,
        in_specs=[VMEM_SPEC] * (1 + len(NEAR)),
        out_specs=VMEM_SPEC,
        compiler_params=params,
        name="relay",
    )(own, *[arrived[offset] for offset in NEAR])
    for distance in relay_shifts(groups):
        known = jnp.maximum(known, shifted(known, distance))

    for mine in ARRIVALS:
        last = mine[-1] == OFFSETS[-1]
        new_cache, attended, *served = pl.pallas_call(
            functools.partial(arrive_kernel, mine, last),
            out_shape=[cache, heads] + [jax.ShapeDtypeStruct((groups,), jnp.int32)] * last,
            in_specs=[VMEM_SPEC] * 3 + [ANY_SPEC] * 2 + [VMEM_SPEC] * (OFFSETS.index(mine[-1]) + 1 + last),
            out_specs=[ANY_SPEC] * (2 + last),
            scratch_shapes=[
                pltpu.VMEM((len(mine),) + stream, kv_cache.dtype),
                pltpu.VMEM((len(mine),) + head_row, queries.dtype),
                pltpu.SemaphoreType.DMA((len(mine), 2)),
            ]
            + [pltpu.VMEM((groups,), jnp.int32), pltpu.SemaphoreType.DMA] * last,
            input_output_aliases={3: 0, 4: 1},
            compiler_params=params,
            name="arrive",
        )(
            own,
            queries,
            fresh_kv,
            new_cache,
            attended,
            *[arrived[offset] for offset in OFFSETS if offset <= mine[-1]],
            *[known] * last,
        )
    return (new_cache, attended, served[0])


def solution(mesh):
    return jax.shard_map(
        per_device,
        mesh=mesh,
        in_specs=(
            P(("rep", "grp")),
            P(("rep", "grp")),
            P(("rep", "grp")),
            P(("rep", "grp"), None, None, "tp"),
            P(("rep", "grp"), None, "tp"),
            P(("rep", "grp"), None, None, "tp"),
        ),
        out_specs=(P(("rep", "grp"), None, None, "tp"), P(("rep", "grp"), None, "tp"), P("rep")),
        check_vma=False,
    )
```

```python
import functools

import jax
import jax.numpy as jnp
from jax import lax
from jax.experimental import pallas as pl
from jax.experimental.pallas import tpu as pltpu
from jax.sharding import PartitionSpec as P

HEAD_DIM = 128
SINK = 4
REACH = 2
STEPS = 2
OFFSETS = tuple(o for o in range(-REACH, REACH + 1) if o != 0)
PACKS = ((-2, -1), (1,), (2,))
NEAR = (-1, -2)
ARRIVALS = ((-2, -1, 1), (2,))
PATCH = 16
LANES = HEAD_DIM
STAY = 0
SENT = 1
POS = SENT + len(OFFSETS)
VMEM_LIMIT = 32 * 1024 * 1024

VMEM_SPEC = pl.BlockSpec(memory_space=pltpu.VMEM)
SMEM_SPEC = pl.BlockSpec(memory_space=pltpu.SMEM)
ANY_SPEC = pl.BlockSpec(memory_space=pl.ANY)
HBM_SPEC = pl.BlockSpec(memory_space=pltpu.HBM)


def shifted(block, distance):
    count = lax.axis_size("grp")
    return lax.ppermute(block, "grp", [(i, (i + distance) % count) for i in range(count)])


def relay_shifts(groups):
    known = {0, *(-o % groups for o in NEAR)}
    late = {-o % groups for o in OFFSETS}
    shifts = []
    while len(known | late) < groups:
        best = max(range(1, groups), key=lambda d: len(known | {(k - d) % groups for k in known} | late))
        known |= {(k - best) % groups for k in known}
        shifts.append(best)
    return shifts


def load_plan(sources, targets, sems):
    copies = [pltpu.make_async_copy(a, b, sems.at[i]) for i, (a, b) in enumerate(zip(sources, targets))]
    for copy in copies:
        copy.start()
    for copy in copies:
        copy.wait()


def row_iota(shape):
    return lax.broadcasted_iota(jnp.int32, shape, 0)


def lane_iota(shape):
    return lax.broadcasted_iota(jnp.int32, shape, len(shape) - 1)


def head_lanes(head):
    return slice(head * HEAD_DIM, (head + 1) * HEAD_DIM)


def first_written(position, cache_len):
    return SINK + lax.rem(position, cache_len - SINK)


def plan_row(hops, live, slots, shape):
    lane = lane_iota(shape)
    stay = jnp.int32(0)
    for s in range(slots):
        stay = stay + jnp.where((s < live) & (hops[s] == 0), 1, 0)
    values = jnp.where(lane == STAY, stay, 0)
    for k, offset in enumerate(OFFSETS):
        sent = jnp.int32(0)
        for s in range(slots):
            sent = jnp.where((s < live) & (hops[s] == offset), 1, sent)
        values = jnp.where(lane == SENT + k, sent, values)
    return values


def pack_kernel(offsets, counts, hops_in, positions_in, kv, *refs):
    blocks = refs[: len(offsets)]
    hops, positions, plan_sems, sems = refs[len(offsets) :]
    load_plan((hops_in, positions_in), (hops, positions), plan_sems)
    slots, _, cache_len, _ = kv.shape
    picks, copies = [], []
    for k, offset in enumerate(offsets):
        pick = jnp.int32(0)
        for s in range(slots):
            pick = jnp.where(hops[s] == offset, s, pick)
        picks.append(pick)
        copies.append(pltpu.make_async_copy(kv.at[pick], blocks[k], sems.at[k]))
        copies[k].start()
    shape = (PATCH, LANES)
    lane, row = lane_iota(shape), row_iota(shape)
    shared = plan_row(hops, counts[0], slots, shape)
    for k in range(len(offsets)):
        position = positions[picks[k]]
        header = jnp.where(lane == POS, position, shared).astype(jnp.float32)
        first = first_written(position, cache_len)
        base = pl.multiple_of((first // PATCH) * PATCH, PATCH)
        copies[k].wait()
        top = blocks[k][0, :PATCH, :LANES].astype(jnp.float32)
        blocks[k][0, :PATCH, :LANES] = jnp.where(row == 0, header, top).astype(jnp.bfloat16)
        patch = blocks[k][0, pl.ds(base, PATCH), :LANES].astype(jnp.float32)
        patch = jnp.where(row == first - base, top[0:1], patch)
        blocks[k][0, pl.ds(base, PATCH), :LANES] = patch.astype(jnp.bfloat16)


def header_of(block):
    return block[0, :PATCH, :LANES].astype(jnp.float32).astype(jnp.int32)


def with_row(table, group, header):
    return jnp.where(row_iota(table.shape) == group, header[0:1], table)


def relay_kernel(own, *refs):
    blocks, table = refs[: len(NEAR)], refs[len(NEAR)]
    groups = table.shape[0]
    here = lax.axis_index("grp")
    rows = with_row(jnp.zeros(table.shape, jnp.int32), here, own[...])
    for offset, block in zip(NEAR, blocks):
        rows = with_row(rows, lax.rem(here - offset + groups, groups), header_of(block))
    table[...] = rows


def attend(old, new, has_header, position, queries, fresh, heads, flush):
    cache_len, width = old.shape[1:]
    head_count = width // HEAD_DIM
    group_size = queries.shape[-1] // width
    first = first_written(position, cache_len)
    second = first_written(position + 1, cache_len)
    for side in range(2):
        written = fresh[side].astype(jnp.float32)
        for head in range(head_count):
            lanes = head_lanes(head)
            rows = old[side, :, lanes].astype(jnp.float32)
            row = row_iota(rows.shape)
            if has_header and (side, head) == (0, 0):
                top = jnp.sum(jnp.where(row == first, rows, 0.0), axis=0, keepdims=True)
                rows = jnp.where(row == 0, top, rows)
            rows = jnp.where(row == second, written[1:2, lanes], jnp.where(row == first, written[0:1, lanes], rows))
            new[side, :, lanes] = rows.astype(jnp.bfloat16)
    flush()

    def both(side, head):
        return jnp.concatenate([new[side, :, head_lanes(head)], old[side, :, head_lanes(head)]], axis=0)

    scores = []
    for head in range(head_count):
        query = jnp.concatenate([queries[:, head_lanes(head * group_size + i)] for i in range(group_size)], axis=0)
        scores.append(
            lax.dot_general(query, both(0, head), (((1,), (1,)), ((), ())), preferred_element_type=jnp.float32)
        )
    scores = jnp.concatenate(scores, axis=0)
    shape = (scores.shape[0], cache_len)
    stale = (row_iota(shape) % STEPS == 0) & (lane_iota(shape) == second)
    scores = jnp.where(stale, scores[:, cache_len:], scores[:, :cache_len]) * HEAD_DIM ** (-0.5)
    weights = jnp.exp(scores - jnp.max(scores, axis=1, keepdims=True))
    weights = weights / jnp.sum(weights, axis=1, keepdims=True)
    weights = jnp.concatenate([jnp.where(stale, 0.0, weights), jnp.where(stale, weights, 0.0)], axis=1)
    weights = weights.astype(jnp.bfloat16)
    for head in range(head_count):
        rows = slice(head * group_size * STEPS, (head + 1) * group_size * STEPS)
        mixed = jnp.dot(weights[rows], both(1, head), preferred_element_type=jnp.float32).astype(jnp.bfloat16)
        for i in range(group_size):
            heads[:, head_lanes(head * group_size + i)] = mixed[i * STEPS : (i + 1) * STEPS]


def stay_kernel(counts, hops_in, positions_in, kv, queries, fresh, cache, attended, own, *scratch):
    hops, positions, plan_sems, buffers, updated, blank, order, load_sems, store_sems = scratch
    load_plan((hops_in, positions_in), (hops, positions), plan_sems)
    slots = kv.shape[0]
    live = counts[0]
    stay = jnp.int32(0)
    for s in range(slots):
        staying = (s < live) & (hops[s] == 0)

        @pl.when(staying)
        def _(s=s, stay=stay):
            order[stay] = s
            pltpu.make_async_copy(kv.at[s], buffers.at[stay], load_sems.at[stay]).start()

        stay = stay + jnp.where(staying, 1, 0)

    own[...] = plan_row(hops, live, slots, own.shape)
    blank[...] = jnp.zeros_like(blank)

    def clear(j, carry):
        pltpu.make_async_copy(blank, cache.at[j], store_sems.at[j]).start()
        attended[j] = jnp.zeros(attended.shape[1:], attended.dtype)
        return carry

    lax.fori_loop(stay, slots, clear, 0)

    def work(j, carry):
        pltpu.make_async_copy(kv.at[0], buffers.at[j], load_sems.at[j]).wait()

        def flush():
            pltpu.make_async_copy(updated.at[j], cache.at[j], store_sems.at[j]).start()

        attend(
            buffers.at[j], updated.at[j], False, positions[order[j]], queries.at[j], fresh.at[j], attended.at[j], flush
        )
        return carry

    lax.fori_loop(0, stay, work, 0)

    def drain(j, carry):
        pltpu.make_async_copy(blank, cache.at[j], store_sems.at[j]).wait()
        return carry

    lax.fori_loop(0, slots, drain, 0)


def arrive_kernel(mine, last, own, queries, fresh, cache_in, attended_in, *refs):
    del cache_in, attended_in
    seen = OFFSETS[: OFFSETS.index(mine[-1]) + 1]
    blocks, refs = dict(zip(seen, refs)), refs[len(seen) :]
    if last:
        known, cache, attended, served, buffers, heads, store_sems, total, total_sem = refs
    else:
        cache, attended, buffers, heads, store_sems = refs
    headers = {offset: header_of(block) for offset, block in blocks.items()}

    def entry(header, lane):
        shape = header[0:1].shape
        return jnp.sum(jnp.where(lane_iota(shape) == lane, header[0:1], 0))

    places = {}
    place = entry(own[...], STAY)
    for k, offset in enumerate(seen):
        present = entry(headers[offset], SENT + k) > 0
        places[offset] = (present, place)
        place = place + jnp.where(present, 1, 0)

    def stores(i, slot):
        return (
            pltpu.make_async_copy(buffers.at[i], cache.at[slot], store_sems.at[i, 0]),
            pltpu.make_async_copy(heads.at[i], attended.at[slot], store_sems.at[i, 1]),
        )

    for i, offset in enumerate(mine):
        present, slot = places[offset]

        @pl.when(present)
        def _(i=i, slot=slot, offset=offset):
            into_cache, into_attended = stores(i, slot)
            position = entry(headers[offset], POS)
            attend(
                blocks[offset],
                buffers.at[i],
                True,
                position,
                queries.at[slot],
                fresh.at[slot],
                heads.at[i],
                into_cache.start,
            )
            into_attended.start()

    if last:
        groups = known.shape[0]
        here = lax.axis_index("grp")
        rows = known[...]
        for offset in OFFSETS:
            rows = with_row(rows, lax.rem(here - offset + groups, groups), headers[offset])
        total[...] = count_served(rows)
        into_served = pltpu.make_async_copy(total, served, total_sem)
        into_served.start()

    for i, offset in enumerate(mine):
        present, slot = places[offset]

        @pl.when(present)
        def _(i=i, slot=slot):
            for copy in stores(i, slot):
                copy.wait()

    if last:
        into_served.wait()


def count_served(rows):
    groups = rows.shape[0]

    def column(lane, shift):
        moved = pltpu.roll(rows, shift % groups, 0) if shift % groups else rows
        return jnp.sum(jnp.where(lane_iota(rows.shape) == lane, moved, 0), axis=1, keepdims=True)

    total = column(STAY, 0)
    for k, offset in enumerate(OFFSETS):
        total = total + column(SENT + k, offset)
    square = (groups, groups)
    return jnp.sum(jnp.where(row_iota(square) == lane_iota(square), total, 0), axis=0)


def per_device(counts, hop_offsets, write_pos, kv_cache, queries, fresh_kv):
    groups = lax.axis_size("grp")
    slots = kv_cache.shape[0]
    stream = kv_cache.shape[1:]
    head_row = queries.shape[1:]
    params = pltpu.CompilerParams(vmem_limit_bytes=VMEM_LIMIT)
    plan = [counts, *(pltpu.with_memory_space_constraint(a, pltpu.HBM) for a in (hop_offsets, write_pos, kv_cache))]
    plan_scratch = [
        pltpu.SMEM(hop_offsets.shape, jnp.int32),
        pltpu.SMEM(write_pos.shape, jnp.int32),
        pltpu.SemaphoreType.DMA((2,)),
    ]
    block = jax.ShapeDtypeStruct(stream, kv_cache.dtype)
    table = jax.ShapeDtypeStruct((groups, LANES), jnp.int32)
    cache = jax.ShapeDtypeStruct(kv_cache.shape, kv_cache.dtype)
    heads = jax.ShapeDtypeStruct(queries.shape, queries.dtype)
    arrived = {}
    for offsets in PACKS:
        blocks = pl.pallas_call(
            functools.partial(pack_kernel, offsets),
            out_shape=[block] * len(offsets),
            in_specs=[SMEM_SPEC] + [HBM_SPEC] * 3,
            out_specs=[VMEM_SPEC] * len(offsets),
            scratch_shapes=plan_scratch + [pltpu.SemaphoreType.DMA((len(offsets),))],
            compiler_params=params,
            name="pack",
        )(*plan)
        for offset, outgoing in zip(offsets, blocks):
            arrived[offset] = shifted(outgoing, offset)

    new_cache, attended, own = pl.pallas_call(
        stay_kernel,
        out_shape=[cache, heads, jax.ShapeDtypeStruct((1, LANES), jnp.int32)],
        in_specs=[SMEM_SPEC] + [HBM_SPEC] * 3 + [VMEM_SPEC, VMEM_SPEC],
        out_specs=[ANY_SPEC, VMEM_SPEC, VMEM_SPEC],
        scratch_shapes=plan_scratch
        + [
            pltpu.VMEM(kv_cache.shape, kv_cache.dtype),
            pltpu.VMEM(kv_cache.shape, kv_cache.dtype),
            pltpu.VMEM(stream, kv_cache.dtype),
            pltpu.SMEM((slots,), jnp.int32),
            pltpu.SemaphoreType.DMA((slots,)),
            pltpu.SemaphoreType.DMA((slots,)),
        ],
        compiler_params=params,
        cost_estimate=pl.CostEstimate(flops=50_000_000, bytes_accessed=4 * kv_cache.size, transcendentals=0),
        name="stay",
    )(*plan, queries, fresh_kv)

    known = pl.pallas_call(
        relay_kernel,
        out_shape=table,
        in_specs=[VMEM_SPEC] * (1 + len(NEAR)),
        out_specs=VMEM_SPEC,
        compiler_params=params,
        name="relay",
    )(own, *[arrived[offset] for offset in NEAR])
    for distance in relay_shifts(groups):
        known = jnp.maximum(known, shifted(known, distance))

    for mine in ARRIVALS:
        last = mine[-1] == OFFSETS[-1]
        new_cache, attended, *served = pl.pallas_call(
            functools.partial(arrive_kernel, mine, last),
            out_shape=[cache, heads] + [jax.ShapeDtypeStruct((groups,), jnp.int32)] * last,
            in_specs=[VMEM_SPEC] * 3 + [ANY_SPEC] * 2 + [VMEM_SPEC] * (OFFSETS.index(mine[-1]) + 1 + last),
            out_specs=[ANY_SPEC] * (2 + last),
            scratch_shapes=[
                pltpu.VMEM((len(mine),) + stream, kv_cache.dtype),
                pltpu.VMEM((len(mine),) + head_row, queries.dtype),
                pltpu.SemaphoreType.DMA((len(mine), 2)),
            ]
            + [pltpu.VMEM((groups,), jnp.int32), pltpu.SemaphoreType.DMA] * last,
            input_output_aliases={3: 0, 4: 1},
            compiler_params=params,
            name="arrive",
        )(
            own,
            queries,
            fresh_kv,
            new_cache,
            attended,
            *[arrived[offset] for offset in OFFSETS if offset <= mine[-1]],
            *[known] * last,
        )
    return (new_cache, attended, served[0])


def solution(mesh):
    return jax.shard_map(
        per_device,
        mesh=mesh,
        in_specs=(
            P(("rep", "grp")),
            P(("rep", "grp")),
            P(("rep", "grp")),
            P(("rep", "grp"), None, None, "tp"),
            P(("rep", "grp"), None, "tp"),
            P(("rep", "grp"), None, None, "tp"),
        ),
        out_specs=(P(("rep", "grp"), None, None, "tp"), P(("rep", "grp"), None, "tp"), P("rep")),
        check_vma=False,
    )
```

```python
import functools

import jax
import jax.numpy as jnp
from jax import lax
from jax.experimental import pallas as pl
from jax.experimental.pallas import tpu as pltpu
from jax.sharding import PartitionSpec as P

HEAD_DIM = 128
SINK = 4
REACH = 2
STEPS = 2
OFFSETS = tuple(o for o in range(-REACH, REACH + 1) if o != 0)
PACKS = ((-2, -1), (1,), (2,))
NEAR = (-1, -2)
ARRIVALS = ((-2, -1, 1), (2,))
PATCH = 16
LANES = HEAD_DIM
STAY = 0
SENT = 1
POS = SENT + len(OFFSETS)
VMEM_LIMIT = 32 * 1024 * 1024

VMEM_SPEC = pl.BlockSpec(memory_space=pltpu.VMEM)
SMEM_SPEC = pl.BlockSpec(memory_space=pltpu.SMEM)
ANY_SPEC = pl.BlockSpec(memory_space=pl.ANY)
HBM_SPEC = pl.BlockSpec(memory_space=pltpu.HBM)


def shifted(block, distance):
    count = lax.axis_size("grp")
    return lax.ppermute(block, "grp", [(i, (i + distance) % count) for i in range(count)])


def relay_shifts(groups):
    known = {0, *(-o % groups for o in NEAR)}
    late = {-o % groups for o in OFFSETS}
    shifts = []
    while len(known | late) < groups:
        best = max(range(1, groups), key=lambda d: len(known | {(k - d) % groups for k in known} | late))
        known |= {(k - best) % groups for k in known}
        shifts.append(best)
    return shifts


def load_plan(sources, targets, sems):
    copies = [pltpu.make_async_copy(a, b, sems.at[i]) for i, (a, b) in enumerate(zip(sources, targets))]
    for copy in copies:
        copy.start()
    for copy in copies:
        copy.wait()


def row_iota(shape):
    return lax.broadcasted_iota(jnp.int32, shape, 0)


def lane_iota(shape):
    return lax.broadcasted_iota(jnp.int32, shape, len(shape) - 1)


def head_lanes(head):
    return slice(head * HEAD_DIM, (head + 1) * HEAD_DIM)


def first_written(position, cache_len):
    return SINK + lax.rem(position, cache_len - SINK)


def plan_row(hops, live, slots, shape):
    lane = lane_iota(shape)
    stay = jnp.int32(0)
    for s in range(slots):
        stay = stay + jnp.where((s < live) & (hops[s] == 0), 1, 0)
    values = jnp.where(lane == STAY, stay, 0)
    for k, offset in enumerate(OFFSETS):
        sent = jnp.int32(0)
        for s in range(slots):
            sent = jnp.where((s < live) & (hops[s] == offset), 1, sent)
        values = jnp.where(lane == SENT + k, sent, values)
    return values


def pack_kernel(offsets, counts, hops_in, positions_in, kv, *refs):
    blocks = refs[: len(offsets)]
    hops, positions, plan_sems, sems = refs[len(offsets) :]
    load_plan((hops_in, positions_in), (hops, positions), plan_sems)
    slots, _, cache_len, _ = kv.shape
    picks, copies = [], []
    for k, offset in enumerate(offsets):
        pick = jnp.int32(0)
        for s in range(slots):
            pick = jnp.where(hops[s] == offset, s, pick)
        picks.append(pick)
        copies.append(pltpu.make_async_copy(kv.at[pick], blocks[k], sems.at[k]))
        copies[k].start()
    shape = (PATCH, LANES)
    lane, row = lane_iota(shape), row_iota(shape)
    shared = plan_row(hops, counts[0], slots, shape)
    for k in range(len(offsets)):
        position = positions[picks[k]]
        header = jnp.where(lane == POS, position, shared).astype(jnp.float32)
        first = first_written(position, cache_len)
        base = pl.multiple_of((first // PATCH) * PATCH, PATCH)
        copies[k].wait()
        top = blocks[k][0, :PATCH, :LANES].astype(jnp.float32)
        blocks[k][0, :PATCH, :LANES] = jnp.where(row == 0, header, top).astype(jnp.bfloat16)
        patch = blocks[k][0, pl.ds(base, PATCH), :LANES].astype(jnp.float32)
        patch = jnp.where(row == first - base, top[0:1], patch)
        blocks[k][0, pl.ds(base, PATCH), :LANES] = patch.astype(jnp.bfloat16)


def header_of(block):
    return block[0, :PATCH, :LANES].astype(jnp.float32).astype(jnp.int32)


def with_row(table, group, header):
    return jnp.where(row_iota(table.shape) == group, header[0:1], table)


def relay_kernel(own, *refs):
    blocks, table = refs[: len(NEAR)], refs[len(NEAR)]
    groups = table.shape[0]
    here = lax.axis_index("grp")
    rows = with_row(jnp.zeros(table.shape, jnp.int32), here, own[...])
    for offset, block in zip(NEAR, blocks):
        rows = with_row(rows, lax.rem(here - offset + groups, groups), header_of(block))
    table[...] = rows


def attend(old, new, has_header, position, queries, fresh, heads, flush):
    cache_len, width = old.shape[1:]
    head_count = width // HEAD_DIM
    group_size = queries.shape[-1] // width
    first = first_written(position, cache_len)
    second = first_written(position + 1, cache_len)
    padding = jnp.zeros((PATCH - STEPS, HEAD_DIM), jnp.bfloat16)
    scores = []
    for head in range(head_count):
        query = jnp.concatenate([queries[:, head_lanes(head * group_size + i)] for i in range(group_size)], axis=0)
        keys = jnp.concatenate([old[0, :, head_lanes(head)], fresh[0][:, head_lanes(head)], padding], axis=0)
        scores.append(lax.dot_general(query, keys, (((1,), (1,)), ((), ())), preferred_element_type=jnp.float32))
    for side in range(2):
        rows_now = fresh[side].astype(jnp.float32)
        for head in range(head_count):
            lanes = head_lanes(head)
            rows = old[side, :, lanes].astype(jnp.float32)
            row = row_iota(rows.shape)
            if has_header and (side, head) == (0, 0):
                top = jnp.sum(jnp.where(row == first, rows, 0.0), axis=0, keepdims=True)
                rows = jnp.where(row == 0, top, rows)
            rows = jnp.where(row == second, rows_now[1:2, lanes], jnp.where(row == first, rows_now[0:1, lanes], rows))
            new[side, :, lanes] = rows.astype(jnp.bfloat16)
    flush()

    def both(side, head):
        return jnp.concatenate([new[side, :, head_lanes(head)], old[side, :, head_lanes(head)]], axis=0)

    scores = jnp.concatenate(scores, axis=0)
    shape = (scores.shape[0], cache_len)
    row, lane = row_iota(shape), lane_iota(shape)
    stale = (row % STEPS == 0) & (lane == second)
    written = [scores[:, cache_len + t : cache_len + t + 1] for t in range(STEPS)]
    scores = scores[:, :cache_len]
    if has_header:
        top = jnp.sum(jnp.where(lane == first, scores, 0.0), axis=1, keepdims=True)
        scores = jnp.where((lane == 0) & (row < group_size * STEPS), top, scores)
    scores = jnp.where(lane == first, written[0], scores)
    scores = jnp.where((lane == second) & jnp.logical_not(stale), written[1], scores) * HEAD_DIM ** (-0.5)
    weights = jnp.exp(scores - jnp.max(scores, axis=1, keepdims=True))
    weights = weights / jnp.sum(weights, axis=1, keepdims=True)
    weights = jnp.concatenate([jnp.where(stale, 0.0, weights), jnp.where(stale, weights, 0.0)], axis=1)
    weights = weights.astype(jnp.bfloat16)
    for head in range(head_count):
        rows = slice(head * group_size * STEPS, (head + 1) * group_size * STEPS)
        mixed = jnp.dot(weights[rows], both(1, head), preferred_element_type=jnp.float32).astype(jnp.bfloat16)
        for i in range(group_size):
            heads[:, head_lanes(head * group_size + i)] = mixed[i * STEPS : (i + 1) * STEPS]


def stay_kernel(counts, hops_in, positions_in, kv, queries, fresh, cache, attended, own, *scratch):
    hops, positions, plan_sems, buffers, updated, blank, order, load_sems, store_sems = scratch
    load_plan((hops_in, positions_in), (hops, positions), plan_sems)
    slots = kv.shape[0]
    live = counts[0]
    stay = jnp.int32(0)
    for s in range(slots):
        staying = (s < live) & (hops[s] == 0)

        @pl.when(staying)
        def _(s=s, stay=stay):
            order[stay] = s
            pltpu.make_async_copy(kv.at[s], buffers.at[stay], load_sems.at[stay]).start()

        stay = stay + jnp.where(staying, 1, 0)

    own[...] = plan_row(hops, live, slots, own.shape)
    blank[...] = jnp.zeros_like(blank)

    def clear(j, carry):
        pltpu.make_async_copy(blank, cache.at[j], store_sems.at[j]).start()
        attended[j] = jnp.zeros(attended.shape[1:], attended.dtype)
        return carry

    lax.fori_loop(stay, slots, clear, 0)

    def work(j, carry):
        pltpu.make_async_copy(kv.at[0], buffers.at[j], load_sems.at[j]).wait()

        def flush():
            pltpu.make_async_copy(updated.at[j], cache.at[j], store_sems.at[j]).start()

        attend(
            buffers.at[j], updated.at[j], False, positions[order[j]], queries.at[j], fresh.at[j], attended.at[j], flush
        )
        return carry

    lax.fori_loop(0, stay, work, 0)

    def drain(j, carry):
        pltpu.make_async_copy(blank, cache.at[j], store_sems.at[j]).wait()
        return carry

    lax.fori_loop(0, slots, drain, 0)


def arrive_kernel(mine, last, own, queries, fresh, cache_in, attended_in, *refs):
    del cache_in, attended_in
    seen = OFFSETS[: OFFSETS.index(mine[-1]) + 1]
    blocks, refs = dict(zip(seen, refs)), refs[len(seen) :]
    if last:
        known, cache, attended, served, buffers, heads, store_sems, total, total_sem = refs
    else:
        cache, attended, buffers, heads, store_sems = refs
    headers = {offset: header_of(block) for offset, block in blocks.items()}

    if last:
        groups = known.shape[0]
        here = lax.axis_index("grp")
        rows = known[...]
        for offset in OFFSETS:
            rows = with_row(rows, lax.rem(here - offset + groups, groups), headers[offset])
        total[...] = count_served(rows)
        into_served = pltpu.make_async_copy(total, served, total_sem)
        into_served.start()

    def entry(header, lane):
        shape = header[0:1].shape
        return jnp.sum(jnp.where(lane_iota(shape) == lane, header[0:1], 0))

    places = {}
    place = entry(own[...], STAY)
    for k, offset in enumerate(seen):
        present = entry(headers[offset], SENT + k) > 0
        places[offset] = (present, place)
        place = place + jnp.where(present, 1, 0)

    def stores(i, slot):
        return (
            pltpu.make_async_copy(buffers.at[i], cache.at[slot], store_sems.at[i, 0]),
            pltpu.make_async_copy(heads.at[i], attended.at[slot], store_sems.at[i, 1]),
        )

    for i, offset in enumerate(mine):
        present, slot = places[offset]

        @pl.when(present)
        def _(i=i, slot=slot, offset=offset):
            into_cache, into_attended = stores(i, slot)
            position = entry(headers[offset], POS)
            attend(
                blocks[offset],
                buffers.at[i],
                True,
                position,
                queries.at[slot],
                fresh.at[slot],
                heads.at[i],
                into_cache.start,
            )
            into_attended.start()

    for i, offset in enumerate(mine):
        present, slot = places[offset]

        @pl.when(present)
        def _(i=i, slot=slot):
            for copy in stores(i, slot):
                copy.wait()

    if last:
        into_served.wait()


def count_served(rows):
    groups = rows.shape[0]

    def column(lane, shift):
        moved = pltpu.roll(rows, shift % groups, 0) if shift % groups else rows
        return jnp.sum(jnp.where(lane_iota(rows.shape) == lane, moved, 0), axis=1, keepdims=True)

    total = column(STAY, 0)
    for k, offset in enumerate(OFFSETS):
        total = total + column(SENT + k, offset)
    square = (groups, groups)
    return jnp.sum(jnp.where(row_iota(square) == lane_iota(square), total, 0), axis=0)


def per_device(counts, hop_offsets, write_pos, kv_cache, queries, fresh_kv):
    groups = lax.axis_size("grp")
    slots = kv_cache.shape[0]
    stream = kv_cache.shape[1:]
    head_row = queries.shape[1:]
    params = pltpu.CompilerParams(vmem_limit_bytes=VMEM_LIMIT)
    plan = [counts, *(pltpu.with_memory_space_constraint(a, pltpu.HBM) for a in (hop_offsets, write_pos, kv_cache))]
    plan_scratch = [
        pltpu.SMEM(hop_offsets.shape, jnp.int32),
        pltpu.SMEM(write_pos.shape, jnp.int32),
        pltpu.SemaphoreType.DMA((2,)),
    ]
    block = jax.ShapeDtypeStruct(stream, kv_cache.dtype)
    table = jax.ShapeDtypeStruct((groups, LANES), jnp.int32)
    cache = jax.ShapeDtypeStruct(kv_cache.shape, kv_cache.dtype)
    heads = jax.ShapeDtypeStruct(queries.shape, queries.dtype)
    arrived = {}
    for offsets in PACKS:
        blocks = pl.pallas_call(
            functools.partial(pack_kernel, offsets),
            out_shape=[block] * len(offsets),
            in_specs=[SMEM_SPEC] + [HBM_SPEC] * 3,
            out_specs=[VMEM_SPEC] * len(offsets),
            scratch_shapes=plan_scratch + [pltpu.SemaphoreType.DMA((len(offsets),))],
            compiler_params=params,
            name="pack",
        )(*plan)
        for offset, outgoing in zip(offsets, blocks):
            arrived[offset] = shifted(outgoing, offset)

    new_cache, attended, own = pl.pallas_call(
        stay_kernel,
        out_shape=[cache, heads, jax.ShapeDtypeStruct((1, LANES), jnp.int32)],
        in_specs=[SMEM_SPEC] + [HBM_SPEC] * 3 + [VMEM_SPEC, VMEM_SPEC],
        out_specs=[ANY_SPEC, VMEM_SPEC, VMEM_SPEC],
        scratch_shapes=plan_scratch
        + [
            pltpu.VMEM(kv_cache.shape, kv_cache.dtype),
            pltpu.VMEM(kv_cache.shape, kv_cache.dtype),
            pltpu.VMEM(stream, kv_cache.dtype),
            pltpu.SMEM((slots,), jnp.int32),
            pltpu.SemaphoreType.DMA((slots,)),
            pltpu.SemaphoreType.DMA((slots,)),
        ],
        compiler_params=params,
        cost_estimate=pl.CostEstimate(flops=50_000_000, bytes_accessed=4 * kv_cache.size, transcendentals=0),
        name="stay",
    )(*plan, queries, fresh_kv)

    known = pl.pallas_call(
        relay_kernel,
        out_shape=table,
        in_specs=[VMEM_SPEC] * (1 + len(NEAR)),
        out_specs=VMEM_SPEC,
        compiler_params=params,
        name="relay",
    )(own, *[arrived[offset] for offset in NEAR])
    for distance in relay_shifts(groups):
        known = jnp.maximum(known, shifted(known, distance))

    for mine in ARRIVALS:
        last = mine[-1] == OFFSETS[-1]
        new_cache, attended, *served = pl.pallas_call(
            functools.partial(arrive_kernel, mine, last),
            out_shape=[cache, heads] + [jax.ShapeDtypeStruct((groups,), jnp.int32)] * last,
            in_specs=[VMEM_SPEC] * 3 + [ANY_SPEC] * 2 + [VMEM_SPEC] * (OFFSETS.index(mine[-1]) + 1 + last),
            out_specs=[ANY_SPEC] * (2 + last),
            scratch_shapes=[
                pltpu.VMEM((len(mine),) + stream, kv_cache.dtype),
                pltpu.VMEM((len(mine),) + head_row, queries.dtype),
                pltpu.SemaphoreType.DMA((len(mine), 2)),
            ]
            + [pltpu.VMEM((groups,), jnp.int32), pltpu.SemaphoreType.DMA] * last,
            input_output_aliases={3: 0, 4: 1},
            compiler_params=params,
            name="arrive",
        )(
            own,
            queries,
            fresh_kv,
            new_cache,
            attended,
            *[arrived[offset] for offset in OFFSETS if offset <= mine[-1]],
            *[known] * last,
        )
    return (new_cache, attended, served[0])


def solution(mesh):
    return jax.shard_map(
        per_device,
        mesh=mesh,
        in_specs=(
            P(("rep", "grp")),
            P(("rep", "grp")),
            P(("rep", "grp")),
            P(("rep", "grp"), None, None, "tp"),
            P(("rep", "grp"), None, "tp"),
            P(("rep", "grp"), None, None, "tp"),
        ),
        out_specs=(P(("rep", "grp"), None, None, "tp"), P(("rep", "grp"), None, "tp"), P("rep")),
        check_vma=False,
    )
```

```python
import functools

import jax
import jax.numpy as jnp
from jax import lax
from jax.experimental import pallas as pl
from jax.experimental.pallas import tpu as pltpu
from jax.sharding import PartitionSpec as P

HEAD_DIM = 128
SINK = 4
REACH = 2
STEPS = 2
OFFSETS = tuple(o for o in range(-REACH, REACH + 1) if o != 0)
PACKS = ((-2, -1), (2,), (1,))
NEAR = (-1, -2)
ARRIVALS = ((-2, -1, 1), (2,))
PATCH = 16
LANES = HEAD_DIM
STAY = 0
SENT = 1
POS = SENT + len(OFFSETS)
VMEM_LIMIT = 32 * 1024 * 1024

VMEM_SPEC = pl.BlockSpec(memory_space=pltpu.VMEM)
SMEM_SPEC = pl.BlockSpec(memory_space=pltpu.SMEM)
ANY_SPEC = pl.BlockSpec(memory_space=pl.ANY)
HBM_SPEC = pl.BlockSpec(memory_space=pltpu.HBM)


def shifted(block, distance):
    count = lax.axis_size("grp")
    return lax.ppermute(block, "grp", [(i, (i + distance) % count) for i in range(count)])


def relay_shifts(groups):
    known = {0, *(-o % groups for o in NEAR)}
    late = {-o % groups for o in OFFSETS}
    shifts = []
    while len(known | late) < groups:
        best = max(range(1, groups), key=lambda d: len(known | {(k - d) % groups for k in known} | late))
        known |= {(k - best) % groups for k in known}
        shifts.append(best)
    return shifts


def load_plan(sources, targets, sems):
    copies = [pltpu.make_async_copy(a, b, sems.at[i]) for i, (a, b) in enumerate(zip(sources, targets))]
    for copy in copies:
        copy.start()
    for copy in copies:
        copy.wait()


def row_iota(shape):
    return lax.broadcasted_iota(jnp.int32, shape, 0)


def lane_iota(shape):
    return lax.broadcasted_iota(jnp.int32, shape, len(shape) - 1)


def head_lanes(head):
    return slice(head * HEAD_DIM, (head + 1) * HEAD_DIM)


def first_written(position, cache_len):
    return SINK + lax.rem(position, cache_len - SINK)


def plan_row(hops, live, slots, shape):
    lane = lane_iota(shape)
    stay = jnp.int32(0)
    for s in range(slots):
        stay = stay + jnp.where((s < live) & (hops[s] == 0), 1, 0)
    values = jnp.where(lane == STAY, stay, 0)
    for k, offset in enumerate(OFFSETS):
        sent = jnp.int32(0)
        for s in range(slots):
            sent = jnp.where((s < live) & (hops[s] == offset), 1, sent)
        values = jnp.where(lane == SENT + k, sent, values)
    return values


def pack_kernel(offsets, counts, hops_in, positions_in, kv, *refs):
    blocks = refs[: len(offsets)]
    hops, positions, plan_sems, sems = refs[len(offsets) :]
    load_plan((hops_in, positions_in), (hops, positions), plan_sems)
    slots, _, cache_len, _ = kv.shape
    picks, copies = [], []
    for k, offset in enumerate(offsets):
        pick = jnp.int32(0)
        for s in range(slots):
            pick = jnp.where(hops[s] == offset, s, pick)
        picks.append(pick)
        copies.append(pltpu.make_async_copy(kv.at[pick], blocks[k], sems.at[k]))
        copies[k].start()
    shape = (PATCH, LANES)
    lane, row = lane_iota(shape), row_iota(shape)
    shared = plan_row(hops, counts[0], slots, shape)
    for k in range(len(offsets)):
        position = positions[picks[k]]
        header = jnp.where(lane == POS, position, shared).astype(jnp.float32)
        first = first_written(position, cache_len)
        base = pl.multiple_of((first // PATCH) * PATCH, PATCH)
        copies[k].wait()
        top = blocks[k][0, :PATCH, :LANES].astype(jnp.float32)
        blocks[k][0, :PATCH, :LANES] = jnp.where(row == 0, header, top).astype(jnp.bfloat16)
        patch = blocks[k][0, pl.ds(base, PATCH), :LANES].astype(jnp.float32)
        patch = jnp.where(row == first - base, top[0:1], patch)
        blocks[k][0, pl.ds(base, PATCH), :LANES] = patch.astype(jnp.bfloat16)


def header_of(block):
    return block[0, :PATCH, :LANES].astype(jnp.float32).astype(jnp.int32)


def with_row(table, group, header):
    return jnp.where(row_iota(table.shape) == group, header[0:1], table)


def relay_kernel(own, *refs):
    blocks, table = refs[: len(NEAR)], refs[len(NEAR)]
    groups = table.shape[0]
    here = lax.axis_index("grp")
    rows = with_row(jnp.zeros(table.shape, jnp.int32), here, own[...])
    for offset, block in zip(NEAR, blocks):
        rows = with_row(rows, lax.rem(here - offset + groups, groups), header_of(block))
    table[...] = rows


def attend(old, new, has_header, position, queries, fresh, heads, flush):
    cache_len, width = old.shape[1:]
    head_count = width // HEAD_DIM
    group_size = queries.shape[-1] // width
    first = first_written(position, cache_len)
    second = first_written(position + 1, cache_len)
    padding = jnp.zeros((PATCH - STEPS, HEAD_DIM), jnp.bfloat16)
    scores = []
    for head in range(head_count):
        query = jnp.concatenate([queries[:, head_lanes(head * group_size + i)] for i in range(group_size)], axis=0)
        keys = jnp.concatenate([old[0, :, head_lanes(head)], fresh[0][:, head_lanes(head)], padding], axis=0)
        scores.append(lax.dot_general(query, keys, (((1,), (1,)), ((), ())), preferred_element_type=jnp.float32))
    for side in range(2):
        rows_now = fresh[side].astype(jnp.float32)
        for head in range(head_count):
            lanes = head_lanes(head)
            rows = old[side, :, lanes].astype(jnp.float32)
            row = row_iota(rows.shape)
            if has_header and (side, head) == (0, 0):
                top = jnp.sum(jnp.where(row == first, rows, 0.0), axis=0, keepdims=True)
                rows = jnp.where(row == 0, top, rows)
            rows = jnp.where(row == second, rows_now[1:2, lanes], jnp.where(row == first, rows_now[0:1, lanes], rows))
            new[side, :, lanes] = rows.astype(jnp.bfloat16)
    flush()

    def both(side, head):
        return jnp.concatenate([new[side, :, head_lanes(head)], old[side, :, head_lanes(head)]], axis=0)

    scores = jnp.concatenate(scores, axis=0)
    shape = (scores.shape[0], cache_len)
    row, lane = row_iota(shape), lane_iota(shape)
    stale = (row % STEPS == 0) & (lane == second)
    written = [scores[:, cache_len + t : cache_len + t + 1] for t in range(STEPS)]
    scores = scores[:, :cache_len]
    if has_header:
        top = jnp.sum(jnp.where(lane == first, scores, 0.0), axis=1, keepdims=True)
        scores = jnp.where((lane == 0) & (row < group_size * STEPS), top, scores)
    scores = jnp.where(lane == first, written[0], scores)
    scores = jnp.where((lane == second) & jnp.logical_not(stale), written[1], scores) * HEAD_DIM ** (-0.5)
    weights = jnp.exp(scores - jnp.max(scores, axis=1, keepdims=True))
    weights = weights / jnp.sum(weights, axis=1, keepdims=True)
    weights = jnp.concatenate([jnp.where(stale, 0.0, weights), jnp.where(stale, weights, 0.0)], axis=1)
    weights = weights.astype(jnp.bfloat16)
    for head in range(head_count):
        rows = slice(head * group_size * STEPS, (head + 1) * group_size * STEPS)
        mixed = jnp.dot(weights[rows], both(1, head), preferred_element_type=jnp.float32).astype(jnp.bfloat16)
        for i in range(group_size):
            heads[:, head_lanes(head * group_size + i)] = mixed[i * STEPS : (i + 1) * STEPS]


def stay_kernel(counts, hops_in, positions_in, kv, queries, fresh, cache, attended, own, *scratch):
    hops, positions, plan_sems, buffers, updated, blank, order, load_sems, store_sems = scratch
    load_plan((hops_in, positions_in), (hops, positions), plan_sems)
    slots = kv.shape[0]
    live = counts[0]
    stay = jnp.int32(0)
    for s in range(slots):
        staying = (s < live) & (hops[s] == 0)

        @pl.when(staying)
        def _(s=s, stay=stay):
            order[stay] = s
            pltpu.make_async_copy(kv.at[s], buffers.at[stay], load_sems.at[stay]).start()

        stay = stay + jnp.where(staying, 1, 0)

    own[...] = plan_row(hops, live, slots, own.shape)
    blank[...] = jnp.zeros_like(blank)

    def clear(j, carry):
        pltpu.make_async_copy(blank, cache.at[j], store_sems.at[j]).start()
        attended[j] = jnp.zeros(attended.shape[1:], attended.dtype)
        return carry

    lax.fori_loop(stay, slots, clear, 0)

    def work(j, carry):
        pltpu.make_async_copy(kv.at[0], buffers.at[j], load_sems.at[j]).wait()

        def flush():
            pltpu.make_async_copy(updated.at[j], cache.at[j], store_sems.at[j]).start()

        attend(
            buffers.at[j], updated.at[j], False, positions[order[j]], queries.at[j], fresh.at[j], attended.at[j], flush
        )
        return carry

    lax.fori_loop(0, stay, work, 0)

    def drain(j, carry):
        pltpu.make_async_copy(blank, cache.at[j], store_sems.at[j]).wait()
        return carry

    lax.fori_loop(0, slots, drain, 0)


def arrive_kernel(mine, last, own, queries, fresh, cache_in, attended_in, *refs):
    del cache_in, attended_in
    seen = OFFSETS[: OFFSETS.index(mine[-1]) + 1]
    blocks, refs = dict(zip(seen, refs)), refs[len(seen) :]
    if last:
        known, cache, attended, served, buffers, heads, store_sems, total, total_sem = refs
    else:
        cache, attended, buffers, heads, store_sems = refs
    headers = {offset: header_of(block) for offset, block in blocks.items()}

    if last:
        groups = known.shape[0]
        here = lax.axis_index("grp")
        rows = known[...]
        for offset in OFFSETS:
            rows = with_row(rows, lax.rem(here - offset + groups, groups), headers[offset])
        total[...] = count_served(rows)
        into_served = pltpu.make_async_copy(total, served, total_sem)
        into_served.start()

    def entry(header, lane):
        shape = header[0:1].shape
        return jnp.sum(jnp.where(lane_iota(shape) == lane, header[0:1], 0))

    places = {}
    place = entry(own[...], STAY)
    for k, offset in enumerate(seen):
        present = entry(headers[offset], SENT + k) > 0
        places[offset] = (present, place)
        place = place + jnp.where(present, 1, 0)

    def stores(i, slot):
        return (
            pltpu.make_async_copy(buffers.at[i], cache.at[slot], store_sems.at[i, 0]),
            pltpu.make_async_copy(heads.at[i], attended.at[slot], store_sems.at[i, 1]),
        )

    for i, offset in enumerate(mine):
        present, slot = places[offset]

        @pl.when(present)
        def _(i=i, slot=slot, offset=offset):
            into_cache, into_attended = stores(i, slot)
            position = entry(headers[offset], POS)
            attend(
                blocks[offset],
                buffers.at[i],
                True,
                position,
                queries.at[slot],
                fresh.at[slot],
                heads.at[i],
                into_cache.start,
            )
            into_attended.start()

    for i, offset in enumerate(mine):
        present, slot = places[offset]

        @pl.when(present)
        def _(i=i, slot=slot):
            for copy in stores(i, slot):
                copy.wait()

    if last:
        into_served.wait()


def count_served(rows):
    groups = rows.shape[0]

    def column(lane, shift):
        moved = pltpu.roll(rows, shift % groups, 0) if shift % groups else rows
        return jnp.sum(jnp.where(lane_iota(rows.shape) == lane, moved, 0), axis=1, keepdims=True)

    total = column(STAY, 0)
    for k, offset in enumerate(OFFSETS):
        total = total + column(SENT + k, offset)
    square = (groups, groups)
    return jnp.sum(jnp.where(row_iota(square) == lane_iota(square), total, 0), axis=0)


def per_device(counts, hop_offsets, write_pos, kv_cache, queries, fresh_kv):
    groups = lax.axis_size("grp")
    slots = kv_cache.shape[0]
    stream = kv_cache.shape[1:]
    head_row = queries.shape[1:]
    params = pltpu.CompilerParams(vmem_limit_bytes=VMEM_LIMIT)
    plan = [counts, *(pltpu.with_memory_space_constraint(a, pltpu.HBM) for a in (hop_offsets, write_pos, kv_cache))]
    plan_scratch = [
        pltpu.SMEM(hop_offsets.shape, jnp.int32),
        pltpu.SMEM(write_pos.shape, jnp.int32),
        pltpu.SemaphoreType.DMA((2,)),
    ]
    block = jax.ShapeDtypeStruct(stream, kv_cache.dtype)
    table = jax.ShapeDtypeStruct((groups, LANES), jnp.int32)
    cache = jax.ShapeDtypeStruct(kv_cache.shape, kv_cache.dtype)
    heads = jax.ShapeDtypeStruct(queries.shape, queries.dtype)
    arrived = {}
    for offsets in PACKS:
        blocks = pl.pallas_call(
            functools.partial(pack_kernel, offsets),
            out_shape=[block] * len(offsets),
            in_specs=[SMEM_SPEC] + [HBM_SPEC] * 3,
            out_specs=[VMEM_SPEC] * len(offsets),
            scratch_shapes=plan_scratch + [pltpu.SemaphoreType.DMA((len(offsets),))],
            compiler_params=params,
            name="pack",
        )(*plan)
        for offset, outgoing in zip(offsets, blocks):
            arrived[offset] = shifted(outgoing, offset)

    new_cache, attended, own = pl.pallas_call(
        stay_kernel,
        out_shape=[cache, heads, jax.ShapeDtypeStruct((1, LANES), jnp.int32)],
        in_specs=[SMEM_SPEC] + [HBM_SPEC] * 3 + [VMEM_SPEC, VMEM_SPEC],
        out_specs=[ANY_SPEC, VMEM_SPEC, VMEM_SPEC],
        scratch_shapes=plan_scratch
        + [
            pltpu.VMEM(kv_cache.shape, kv_cache.dtype),
            pltpu.VMEM(kv_cache.shape, kv_cache.dtype),
            pltpu.VMEM(stream, kv_cache.dtype),
            pltpu.SMEM((slots,), jnp.int32),
            pltpu.SemaphoreType.DMA((slots,)),
            pltpu.SemaphoreType.DMA((slots,)),
        ],
        compiler_params=params,
        cost_estimate=pl.CostEstimate(flops=50_000_000, bytes_accessed=4 * kv_cache.size, transcendentals=0),
        name="stay",
    )(*plan, queries, fresh_kv)

    known = pl.pallas_call(
        relay_kernel,
        out_shape=table,
        in_specs=[VMEM_SPEC] * (1 + len(NEAR)),
        out_specs=VMEM_SPEC,
        compiler_params=params,
        name="relay",
    )(own, *[arrived[offset] for offset in NEAR])
    for distance in relay_shifts(groups):
        known = jnp.maximum(known, shifted(known, distance))

    for mine in ARRIVALS:
        last = mine[-1] == OFFSETS[-1]
        new_cache, attended, *served = pl.pallas_call(
            functools.partial(arrive_kernel, mine, last),
            out_shape=[cache, heads] + [jax.ShapeDtypeStruct((groups,), jnp.int32)] * last,
            in_specs=[VMEM_SPEC] * 3 + [ANY_SPEC] * 2 + [VMEM_SPEC] * (OFFSETS.index(mine[-1]) + 1 + last),
            out_specs=[ANY_SPEC] * (2 + last),
            scratch_shapes=[
                pltpu.VMEM((len(mine),) + stream, kv_cache.dtype),
                pltpu.VMEM((len(mine),) + head_row, queries.dtype),
                pltpu.SemaphoreType.DMA((len(mine), 2)),
            ]
            + [pltpu.VMEM((groups,), jnp.int32), pltpu.SemaphoreType.DMA] * last,
            input_output_aliases={3: 0, 4: 1},
            compiler_params=params,
            name="arrive",
        )(
            own,
            queries,
            fresh_kv,
            new_cache,
            attended,
            *[arrived[offset] for offset in OFFSETS if offset <= mine[-1]],
            *[known] * last,
        )
    return (new_cache, attended, served[0])


def solution(mesh):
    return jax.shard_map(
        per_device,
        mesh=mesh,
        in_specs=(
            P(("rep", "grp")),
            P(("rep", "grp")),
            P(("rep", "grp")),
            P(("rep", "grp"), None, None, "tp"),
            P(("rep", "grp"), None, "tp"),
            P(("rep", "grp"), None, None, "tp"),
        ),
        out_specs=(P(("rep", "grp"), None, None, "tp"), P(("rep", "grp"), None, "tp"), P("rep")),
        check_vma=False,
    )
```

```python
import functools

import jax
import jax.numpy as jnp
from jax import lax
from jax.experimental import pallas as pl
from jax.experimental.pallas import tpu as pltpu
from jax.sharding import PartitionSpec as P

HEAD_DIM = 128
SINK = 4
REACH = 2
STEPS = 2
OFFSETS = tuple(o for o in range(-REACH, REACH + 1) if o != 0)
PACKS = ((-1, -2), (2,), (1,))
NEAR = (-1, -2)
ARRIVALS = ((-2, -1, 1), (2,))
PATCH = 16
LANES = HEAD_DIM
STAY = 0
SENT = 1
POS = SENT + len(OFFSETS)
VMEM_LIMIT = 32 * 1024 * 1024

VMEM_SPEC = pl.BlockSpec(memory_space=pltpu.VMEM)
SMEM_SPEC = pl.BlockSpec(memory_space=pltpu.SMEM)
ANY_SPEC = pl.BlockSpec(memory_space=pl.ANY)
HBM_SPEC = pl.BlockSpec(memory_space=pltpu.HBM)


def shifted(block, distance):
    count = lax.axis_size("grp")
    return lax.ppermute(block, "grp", [(i, (i + distance) % count) for i in range(count)])


def relay_shifts(groups):
    known = {0, *(-o % groups for o in NEAR)}
    late = {-o % groups for o in OFFSETS}
    shifts = []
    while len(known | late) < groups:
        best = max(range(1, groups), key=lambda d: len(known | {(k - d) % groups for k in known} | late))
        known |= {(k - best) % groups for k in known}
        shifts.append(best)
    return shifts


def load_plan(sources, targets, sems):
    copies = [pltpu.make_async_copy(a, b, sems.at[i]) for i, (a, b) in enumerate(zip(sources, targets))]
    for copy in copies:
        copy.start()
    for copy in copies:
        copy.wait()


def row_iota(shape):
    return lax.broadcasted_iota(jnp.int32, shape, 0)


def lane_iota(shape):
    return lax.broadcasted_iota(jnp.int32, shape, len(shape) - 1)


def head_lanes(head):
    return slice(head * HEAD_DIM, (head + 1) * HEAD_DIM)


def first_written(position, cache_len):
    return SINK + lax.rem(position, cache_len - SINK)


def plan_row(hops, live, slots, shape):
    lane = lane_iota(shape)
    stay = jnp.int32(0)
    for s in range(slots):
        stay = stay + jnp.where((s < live) & (hops[s] == 0), 1, 0)
    values = jnp.where(lane == STAY, stay, 0)
    for k, offset in enumerate(OFFSETS):
        sent = jnp.int32(0)
        for s in range(slots):
            sent = jnp.where((s < live) & (hops[s] == offset), 1, sent)
        values = jnp.where(lane == SENT + k, sent, values)
    return values


def pack_kernel(offsets, counts, hops_in, positions_in, kv, *refs):
    blocks = refs[: len(offsets)]
    hops, positions, plan_sems, sems = refs[len(offsets) :]
    load_plan((hops_in, positions_in), (hops, positions), plan_sems)
    slots, _, cache_len, _ = kv.shape
    picks, copies = [], []
    for k, offset in enumerate(offsets):
        pick = jnp.int32(0)
        for s in range(slots):
            pick = jnp.where(hops[s] == offset, s, pick)
        picks.append(pick)
        copies.append(pltpu.make_async_copy(kv.at[pick], blocks[k], sems.at[k]))
        copies[k].start()
    shape = (PATCH, LANES)
    lane, row = lane_iota(shape), row_iota(shape)
    shared = plan_row(hops, counts[0], slots, shape)
    for k in range(len(offsets)):
        position = positions[picks[k]]
        header = jnp.where(lane == POS, position, shared).astype(jnp.float32)
        first = first_written(position, cache_len)
        base = pl.multiple_of((first // PATCH) * PATCH, PATCH)
        copies[k].wait()
        top = blocks[k][0, :PATCH, :LANES].astype(jnp.float32)
        blocks[k][0, :PATCH, :LANES] = jnp.where(row == 0, header, top).astype(jnp.bfloat16)
        patch = blocks[k][0, pl.ds(base, PATCH), :LANES].astype(jnp.float32)
        patch = jnp.where(row == first - base, top[0:1], patch)
        blocks[k][0, pl.ds(base, PATCH), :LANES] = patch.astype(jnp.bfloat16)


def header_of(block):
    return block[0, :PATCH, :LANES].astype(jnp.float32).astype(jnp.int32)


def with_row(table, group, header):
    return jnp.where(row_iota(table.shape) == group, header[0:1], table)


def relay_kernel(own, *refs):
    blocks, table = refs[: len(NEAR)], refs[len(NEAR)]
    groups = table.shape[0]
    here = lax.axis_index("grp")
    rows = with_row(jnp.zeros(table.shape, jnp.int32), here, own[...])
    for offset, block in zip(NEAR, blocks):
        rows = with_row(rows, lax.rem(here - offset + groups, groups), header_of(block))
    table[...] = rows


def attend(old, new, has_header, position, queries, fresh, heads, flush):
    cache_len, width = old.shape[1:]
    head_count = width // HEAD_DIM
    group_size = queries.shape[-1] // width
    first = first_written(position, cache_len)
    second = first_written(position + 1, cache_len)
    padding = jnp.zeros((PATCH - STEPS, HEAD_DIM), jnp.bfloat16)
    scores = []
    for head in range(head_count):
        query = jnp.concatenate([queries[:, head_lanes(head * group_size + i)] for i in range(group_size)], axis=0)
        keys = jnp.concatenate([old[0, :, head_lanes(head)], fresh[0][:, head_lanes(head)], padding], axis=0)
        scores.append(lax.dot_general(query, keys, (((1,), (1,)), ((), ())), preferred_element_type=jnp.float32))
    for side in range(2):
        rows_now = fresh[side].astype(jnp.float32)
        for head in range(head_count):
            lanes = head_lanes(head)
            rows = old[side, :, lanes].astype(jnp.float32)
            row = row_iota(rows.shape)
            if has_header and (side, head) == (0, 0):
                top = jnp.sum(jnp.where(row == first, rows, 0.0), axis=0, keepdims=True)
                rows = jnp.where(row == 0, top, rows)
            rows = jnp.where(row == second, rows_now[1:2, lanes], jnp.where(row == first, rows_now[0:1, lanes], rows))
            new[side, :, lanes] = rows.astype(jnp.bfloat16)
    flush()

    def both(side, head):
        return jnp.concatenate([new[side, :, head_lanes(head)], old[side, :, head_lanes(head)]], axis=0)

    scores = jnp.concatenate(scores, axis=0)
    shape = (scores.shape[0], cache_len)
    row, lane = row_iota(shape), lane_iota(shape)
    stale = (row % STEPS == 0) & (lane == second)
    written = [scores[:, cache_len + t : cache_len + t + 1] for t in range(STEPS)]
    scores = scores[:, :cache_len]
    if has_header:
        top = jnp.sum(jnp.where(lane == first, scores, 0.0), axis=1, keepdims=True)
        scores = jnp.where((lane == 0) & (row < group_size * STEPS), top, scores)
    scores = jnp.where(lane == first, written[0], scores)
    scores = jnp.where((lane == second) & jnp.logical_not(stale), written[1], scores) * HEAD_DIM ** (-0.5)
    weights = jnp.exp(scores - jnp.max(scores, axis=1, keepdims=True))
    weights = weights / jnp.sum(weights, axis=1, keepdims=True)
    weights = jnp.concatenate([jnp.where(stale, 0.0, weights), jnp.where(stale, weights, 0.0)], axis=1)
    weights = weights.astype(jnp.bfloat16)
    for head in range(head_count):
        rows = slice(head * group_size * STEPS, (head + 1) * group_size * STEPS)
        mixed = jnp.dot(weights[rows], both(1, head), preferred_element_type=jnp.float32).astype(jnp.bfloat16)
        for i in range(group_size):
            heads[:, head_lanes(head * group_size + i)] = mixed[i * STEPS : (i + 1) * STEPS]


def stay_kernel(counts, hops_in, positions_in, kv, queries, fresh, cache, attended, own, *scratch):
    hops, positions, plan_sems, buffers, updated, blank, order, load_sems, store_sems = scratch
    load_plan((hops_in, positions_in), (hops, positions), plan_sems)
    slots = kv.shape[0]
    live = counts[0]
    stay = jnp.int32(0)
    for s in range(slots):
        staying = (s < live) & (hops[s] == 0)

        @pl.when(staying)
        def _(s=s, stay=stay):
            order[stay] = s
            pltpu.make_async_copy(kv.at[s], buffers.at[stay], load_sems.at[stay]).start()

        stay = stay + jnp.where(staying, 1, 0)

    own[...] = plan_row(hops, live, slots, own.shape)
    blank[...] = jnp.zeros_like(blank)

    def clear(j, carry):
        pltpu.make_async_copy(blank, cache.at[j], store_sems.at[j]).start()
        attended[j] = jnp.zeros(attended.shape[1:], attended.dtype)
        return carry

    lax.fori_loop(stay, slots, clear, 0)

    def work(j, carry):
        pltpu.make_async_copy(kv.at[0], buffers.at[j], load_sems.at[j]).wait()

        def flush():
            pltpu.make_async_copy(updated.at[j], cache.at[j], store_sems.at[j]).start()

        attend(
            buffers.at[j], updated.at[j], False, positions[order[j]], queries.at[j], fresh.at[j], attended.at[j], flush
        )
        return carry

    lax.fori_loop(0, stay, work, 0)

    def drain(j, carry):
        pltpu.make_async_copy(blank, cache.at[j], store_sems.at[j]).wait()
        return carry

    lax.fori_loop(0, slots, drain, 0)


def arrive_kernel(mine, last, own, queries, fresh, cache_in, attended_in, *refs):
    del cache_in, attended_in
    seen = OFFSETS[: OFFSETS.index(mine[-1]) + 1]
    blocks, refs = dict(zip(seen, refs)), refs[len(seen) :]
    if last:
        known, cache, attended, served, buffers, heads, store_sems, total, total_sem = refs
    else:
        cache, attended, buffers, heads, store_sems = refs
    headers = {offset: header_of(block) for offset, block in blocks.items()}

    if last:
        groups = known.shape[0]
        here = lax.axis_index("grp")
        rows = known[...]
        for offset in OFFSETS:
            rows = with_row(rows, lax.rem(here - offset + groups, groups), headers[offset])
        total[...] = count_served(rows)
        into_served = pltpu.make_async_copy(total, served, total_sem)
        into_served.start()

    def entry(header, lane):
        shape = header[0:1].shape
        return jnp.sum(jnp.where(lane_iota(shape) == lane, header[0:1], 0))

    places = {}
    place = entry(own[...], STAY)
    for k, offset in enumerate(seen):
        present = entry(headers[offset], SENT + k) > 0
        places[offset] = (present, place)
        place = place + jnp.where(present, 1, 0)

    def stores(i, slot):
        return (
            pltpu.make_async_copy(buffers.at[i], cache.at[slot], store_sems.at[i, 0]),
            pltpu.make_async_copy(heads.at[i], attended.at[slot], store_sems.at[i, 1]),
        )

    for i, offset in enumerate(mine):
        present, slot = places[offset]

        @pl.when(present)
        def _(i=i, slot=slot, offset=offset):
            into_cache, into_attended = stores(i, slot)
            position = entry(headers[offset], POS)
            attend(
                blocks[offset],
                buffers.at[i],
                True,
                position,
                queries.at[slot],
                fresh.at[slot],
                heads.at[i],
                into_cache.start,
            )
            into_attended.start()

    for i, offset in enumerate(mine):
        present, slot = places[offset]

        @pl.when(present)
        def _(i=i, slot=slot):
            for copy in stores(i, slot):
                copy.wait()

    if last:
        into_served.wait()


def count_served(rows):
    groups = rows.shape[0]

    def column(lane, shift):
        moved = pltpu.roll(rows, shift % groups, 0) if shift % groups else rows
        return jnp.sum(jnp.where(lane_iota(rows.shape) == lane, moved, 0), axis=1, keepdims=True)

    total = column(STAY, 0)
    for k, offset in enumerate(OFFSETS):
        total = total + column(SENT + k, offset)
    square = (groups, groups)
    return jnp.sum(jnp.where(row_iota(square) == lane_iota(square), total, 0), axis=0)


def per_device(counts, hop_offsets, write_pos, kv_cache, queries, fresh_kv):
    groups = lax.axis_size("grp")
    slots = kv_cache.shape[0]
    stream = kv_cache.shape[1:]
    head_row = queries.shape[1:]
    params = pltpu.CompilerParams(vmem_limit_bytes=VMEM_LIMIT)
    plan = [counts, *(pltpu.with_memory_space_constraint(a, pltpu.HBM) for a in (hop_offsets, write_pos, kv_cache))]
    plan_scratch = [
        pltpu.SMEM(hop_offsets.shape, jnp.int32),
        pltpu.SMEM(write_pos.shape, jnp.int32),
        pltpu.SemaphoreType.DMA((2,)),
    ]
    block = jax.ShapeDtypeStruct(stream, kv_cache.dtype)
    table = jax.ShapeDtypeStruct((groups, LANES), jnp.int32)
    cache = jax.ShapeDtypeStruct(kv_cache.shape, kv_cache.dtype)
    heads = jax.ShapeDtypeStruct(queries.shape, queries.dtype)
    arrived = {}
    for offsets in PACKS:
        blocks = pl.pallas_call(
            functools.partial(pack_kernel, offsets),
            out_shape=[block] * len(offsets),
            in_specs=[SMEM_SPEC] + [HBM_SPEC] * 3,
            out_specs=[VMEM_SPEC] * len(offsets),
            scratch_shapes=plan_scratch + [pltpu.SemaphoreType.DMA((len(offsets),))],
            compiler_params=params,
            name="pack",
        )(*plan)
        for offset, outgoing in zip(offsets, blocks):
            arrived[offset] = shifted(outgoing, offset)

    new_cache, attended, own = pl.pallas_call(
        stay_kernel,
        out_shape=[cache, heads, jax.ShapeDtypeStruct((1, LANES), jnp.int32)],
        in_specs=[SMEM_SPEC] + [HBM_SPEC] * 3 + [VMEM_SPEC, VMEM_SPEC],
        out_specs=[ANY_SPEC, VMEM_SPEC, VMEM_SPEC],
        scratch_shapes=plan_scratch
        + [
            pltpu.VMEM(kv_cache.shape, kv_cache.dtype),
            pltpu.VMEM(kv_cache.shape, kv_cache.dtype),
            pltpu.VMEM(stream, kv_cache.dtype),
            pltpu.SMEM((slots,), jnp.int32),
            pltpu.SemaphoreType.DMA((slots,)),
            pltpu.SemaphoreType.DMA((slots,)),
        ],
        compiler_params=params,
        cost_estimate=pl.CostEstimate(flops=50_000_000, bytes_accessed=4 * kv_cache.size, transcendentals=0),
        name="stay",
    )(*plan, queries, fresh_kv)

    known = pl.pallas_call(
        relay_kernel,
        out_shape=table,
        in_specs=[VMEM_SPEC] * (1 + len(NEAR)),
        out_specs=VMEM_SPEC,
        compiler_params=params,
        name="relay",
    )(own, *[arrived[offset] for offset in NEAR])
    for distance in relay_shifts(groups):
        known = jnp.maximum(known, shifted(known, distance))

    for mine in ARRIVALS:
        last = mine[-1] == OFFSETS[-1]
        new_cache, attended, *served = pl.pallas_call(
            functools.partial(arrive_kernel, mine, last),
            out_shape=[cache, heads] + [jax.ShapeDtypeStruct((groups,), jnp.int32)] * last,
            in_specs=[VMEM_SPEC] * 3 + [ANY_SPEC] * 2 + [VMEM_SPEC] * (OFFSETS.index(mine[-1]) + 1 + last),
            out_specs=[ANY_SPEC] * (2 + last),
            scratch_shapes=[
                pltpu.VMEM((len(mine),) + stream, kv_cache.dtype),
                pltpu.VMEM((len(mine),) + head_row, queries.dtype),
                pltpu.SemaphoreType.DMA((len(mine), 2)),
            ]
            + [pltpu.VMEM((groups,), jnp.int32), pltpu.SemaphoreType.DMA] * last,
            input_output_aliases={3: 0, 4: 1},
            compiler_params=params,
            name="arrive",
        )(
            own,
            queries,
            fresh_kv,
            new_cache,
            attended,
            *[arrived[offset] for offset in OFFSETS if offset <= mine[-1]],
            *[known] * last,
        )
    return (new_cache, attended, served[0])


def solution(mesh):
    return jax.shard_map(
        per_device,
        mesh=mesh,
        in_specs=(
            P(("rep", "grp")),
            P(("rep", "grp")),
            P(("rep", "grp")),
            P(("rep", "grp"), None, None, "tp"),
            P(("rep", "grp"), None, "tp"),
            P(("rep", "grp"), None, None, "tp"),
        ),
        out_specs=(P(("rep", "grp"), None, None, "tp"), P(("rep", "grp"), None, "tp"), P("rep")),
        check_vma=False,
    )
```
